128 devices in a mesh: cp: 16 (over x, y), sc: 8 (over z, core).
Axes of the slice: x: 4, y: 4, z: 4, core: 2. Of those that a mesh axis runs over, the one named last changes fastest.
Arguments:
- factors: bfloat16 [32768, 256], P('sc'), may hold values from -6 to 6
- loadings: bfloat16 [65536, 256], P('cp'), may hold values from -0.375 to 0.375
- thresholds: bfloat16 [65536], P('cp'), may hold values from -2.5 to -0.5
- exposures: bfloat16 [65536, 8], P('cp'), may hold values from 0.099609375 to 1
- aversion: float32 [8], replicated, may hold values from 20 to 2000
- lengths: int32 [16], replicated, may hold values from 1 to 4096, 32768 in all
Outputs:
- grad_load: float32 [65536, 256], P('cp', 'sc')
- grad_thresh: float32 [65536], P('cp')
- grad_expo: float32 [65536, 8], P('cp')
- risk: float32 [8], replicated
The draws below stay inside these ranges and needn't reach their ends.
Inputs may be any that keep to these rules, and one draw needn't show every extreme that they name: `lengths`: each entry counts the live counterparties at the head of its block of 4096 slots; they sum to 32768 and the largest is exactly 4096.
All inputs are finite; a program needn't handle non-finite values.
Results may differ from the reference program's by a relative error of at most 0.0041.
Values may be sent and summed in bfloat16 or wider, within the bound.
A program may use at most 256 MiB of HBM per device.

```python
import math
import jax
import jax.numpy as jnp
import numpy as np
from jax import lax

F = 256
DATES = 8
ROW_DEV = 4096
S_ALL = 32768
ROWS = 65536
LIVE = 32768
N_CP = 16


def level_of(rng, shape, pieces, least, largest):
    def one(position, shards_of):
        steps = jax.random.uniform(jax.random.fold_in(jax.random.fold_in(rng, 6), position), (shards_of,), jnp.float32, least / len(pieces), largest / len(pieces))
        return jnp.repeat(jnp.exp(steps), shape[position] // shards_of).reshape((-1,) + (1,) * (len(shape) - position - 1))

    factor_of = one(*pieces[0])
    for cut in pieces[1:]:
        factor_of = factor_of * one(*cut)
    return factor_of


def split_up(count, total, reach, lean):
    portions = [(1 << 20) // math.isqrt(grade ** lean) + 1 for grade in range(2, count + 1)]
    rest, counts = total - reach - (count - 1), [1] * (count - 1)
    while rest > 0:
        free = [i for i in range(count - 1) if counts[i] < reach]
        mass, left = sum([portions[i] for i in free]), rest
        for i in free:
            more = min(reach - counts[i], max(1, left * portions[i] // mass), rest)
            counts[i] = counts[i] + more
            rest = rest - more
    return np.array([reach] + counts)


def uneven_parts(rng, number_of, total, bound, lean):
    if number_of == 2:
        one = jax.random.randint(rng, (), max(1, total - bound), min(bound, total - 1) + 1)
        return jnp.stack([one, total - one])
    sizes = jnp.asarray(split_up(number_of, total, bound, lean), jnp.int32)
    couples = (number_of - 1) // 2
    source_of, receiver = sizes[1:1 + 2 * couples:2], sizes[2:2 + 2 * couples:2]
    room = jnp.minimum(source_of - 1, bound - receiver)
    passed = jax.random.randint(jax.random.fold_in(rng, 1), (couples,), 0, 1 << 20) % (room + 1)
    sizes = sizes.at[1:1 + 2 * couples:2].set(source_of - passed).at[2:2 + 2 * couples:2].set(receiver + passed)
    return sizes[jax.random.permutation(jax.random.fold_in(rng, 2), number_of)]


def normal_values(own_key, shape, spread, reach, pieces=(), kind=jnp.bfloat16):
    factor_of = level_of(own_key, shape, pieces, -0.22, 0.18) if pieces else 1.0
    array = jax.random.normal(own_key, shape, jnp.float32) * spread * factor_of
    return jnp.minimum(jnp.maximum(array, -reach), reach).astype(kind)


def setup_inputs(seed: int = 0) -> dict:
    seeds = jax.random.split(jax.random.key(seed), 7)
    return {
        "factors": normal_values(seeds[0], (S_ALL, F), 1.0, 6.0, ((0, 8),)),
        "loadings": normal_values(seeds[1], (ROWS, F), F ** -0.5, 0.375, ((0, 16),)),
        "thresholds": jnp.clip(-2.5 + 2.0 * jax.random.uniform(seeds[2], (ROWS,), jnp.float32) ** level_of(seeds[2], (ROWS,), ((0, 16),), -0.2, 0.2), -2.5, -0.5).astype(jnp.bfloat16),
        "exposures": jnp.clip(jnp.exp(math.log(1.0) - 2.306499 * jax.random.uniform(seeds[3], (ROWS, DATES), jnp.float32) ** level_of(seeds[3], (ROWS, DATES), ((0, 16),), -0.2, 0.2)), 0.099609375, 1.0).astype(jnp.bfloat16),
        "aversion": jnp.clip(jnp.exp(jax.random.uniform(seeds[4], (DATES,), jnp.float32, math.log(20.0), math.log(2000.0))), 20.0, 2000.0),
        "lengths": uneven_parts(seeds[5], N_CP, LIVE, ROW_DEV, 2).astype(jnp.int32),
    }


INV_ROOT_TWO = 0.7071067811865476
INV_ROOT_TWOPI = 0.3989422804014327

def normal_cdf(values):
    return 0.5 * lax.erfc(-values * INV_ROOT_TWO)

def normal_pdf(values):
    return INV_ROOT_TWOPI * jnp.exp(-0.5 * values * values)

def reference(factors, loadings, thresholds, exposures, aversion, lengths):
    load_blocks = loadings.reshape(N_CP, ROW_DEV, F)
    limit_blocks = thresholds.reshape(N_CP, ROW_DEV)
    expo_blocks = exposures.reshape(N_CP, ROW_DEV, DATES)
    positions = jnp.arange(ROW_DEV, dtype=jnp.int32)

    def forward(load_rows, limit_rows, expo_rows, live_rows):
        live_mask = (positions < live_rows).astype(jnp.float32)
        project = jnp.dot(factors, load_rows.T, preferred_element_type=jnp.float32)
        loads32 = load_rows.astype(jnp.float32)
        scaled = jnp.sqrt(1.0 + lax.optimization_barrier(jnp.sum(loads32 * loads32, axis=1)))
        latent = (limit_rows.astype(jnp.float32)[None, :] - project) / scaled[None, :]
        probab = (live_mask[None, :] * normal_cdf(latent)).astype(jnp.bfloat16)
        partial_loss = jnp.dot(probab, expo_rows, preferred_element_type=jnp.float32)
        return (live_mask, scaled, latent, probab, partial_loss)

    def add_loss(state, inputs):
        outputs = forward(*inputs)
        return (state + outputs[4], None)
    loss_sum, unused = lax.scan(add_loss, jnp.zeros((S_ALL, DATES), jnp.float32), (load_blocks, limit_blocks, expo_blocks, lengths))
    scores = aversion[None, :] * (loss_sum / LIVE)
    top_score = lax.optimization_barrier(jnp.max(scores, axis=0))
    expd = jnp.exp(scores - top_score[None, :])
    total_mass = lax.optimization_barrier(jnp.sum(expd, axis=0))
    risk = (top_score + jnp.log(total_mass / S_ALL)) / aversion
    weights = (expd / total_mass[None, :]).astype(jnp.bfloat16)

    def gradients(inputs):
        load_rows, limit_rows, expo_rows, live_rows = inputs
        live_mask, scaled, latent, probab, unused_loss = forward(load_rows, limit_rows, expo_rows, live_rows)
        pull_grad = jnp.dot(weights, expo_rows.T, preferred_element_type=jnp.float32) * (live_mask / LIVE)[None, :]
        heavy_grad = pull_grad * normal_pdf(latent)
        load_part = jnp.dot(heavy_grad.astype(jnp.bfloat16).T, factors, preferred_element_type=jnp.float32)
        lat_part = lax.optimization_barrier(jnp.sum(heavy_grad * latent, axis=0))
        thr_part = lax.optimization_barrier(jnp.sum(heavy_grad, axis=0))
        expo_part = jnp.dot(probab.T, weights, preferred_element_type=jnp.float32) / LIVE
        loads32 = load_rows.astype(jnp.float32)
        grad_load = -load_part / scaled[:, None] - (lat_part / (scaled * scaled))[:, None] * loads32
        grad_thresh = thr_part / scaled
        return (grad_load, grad_thresh, expo_part)
    grad_load, grad_thresh, grad_expo = lax.map(gradients, (load_blocks, limit_blocks, expo_blocks, lengths))
    return (grad_load.reshape(ROWS, F), grad_thresh.reshape(ROWS), grad_expo.reshape(ROWS, DATES), risk)
```

```python
import functools
import math

import jax
import jax.numpy as jnp
from jax import lax
from jax.experimental import pallas as pl
from jax.experimental.pallas import tpu as pltpu
from jax.sharding import PartitionSpec as P

MESH = pl.DeviceIdType.MESH
NCP = 16
NSC = 8
F = 256
ROWS = 4096
S = 4096
CAP = 2176
SEG = ROWS // NCP
LIVE = 32768
SCEN = 32768
ST = 512
CHUNK = 544
ROOT_HALF = 0.7071067811865476
LOG2E = 1.4426950408889634
FAR = -3.1
TAIL = (-0.750217616, 0.756257034, -1.37553279, 0.0025935648)
BF = jnp.bfloat16
F32 = jnp.float32


def spots(lengths_ref, position):
    start = jnp.int32(0)
    out = []
    for block in range(NCP):
        live = lengths_ref[block]
        tiles = (live + 15) // 16
        offset = (position - block + NCP) % NCP
        out.append((start, offset, live))
        start = start + (tiles - offset + 15) // 16
    return out


def exchange_kernel(tiles, small, got, got_small, sends, recvs, sends_s, recvs_s, sends_b, recvs_b, own):
    me = lax.axis_index("cp")
    sc = lax.axis_index("sc")
    core = sc % 2
    sibling = sc + 1 - 2 * core
    barrier = pltpu.get_barrier_semaphore()

    def greet(k, _):
        pl.semaphore_signal(barrier, inc=1, device_id=((me + k) % NCP, sc), device_id_type=MESH)
        return 0

    lax.fori_loop(1, NCP, greet, 0)
    pl.semaphore_signal(barrier, inc=1, device_id=(me, sibling), device_id_type=MESH)
    pl.semaphore_wait(barrier, NCP)

    half = pl.ds(core * 8, 8)

    def row_copy(k):
        peer = (me + k) % NCP
        return pltpu.make_async_remote_copy(
            src_ref=tiles.at[half, (peer - me + NCP) % NCP],
            dst_ref=got.at[me, half],
            send_sem=sends.at[k],
            recv_sem=recvs.at[k],
            device_id=(peer, sc),
            device_id_type=MESH,
        )

    def small_copy(k):
        peer = (me + k) % NCP
        return pltpu.make_async_remote_copy(
            src_ref=small.at[(peer - me + NCP) % NCP],
            dst_ref=got_small.at[me],
            send_sem=sends_s.at[k],
            recv_sem=recvs_s.at[k],
            device_id=(peer, sc),
            device_id_type=MESH,
        )

    def forward(k):
        source = (me - k + NCP) % NCP
        return pltpu.make_async_remote_copy(
            src_ref=got.at[source, half],
            dst_ref=got.at[source, half],
            send_sem=sends_b.at[k],
            recv_sem=recvs_b.at[k],
            device_id=(me, sibling),
            device_id_type=MESH,
        )

    def start(k, _):
        row_copy(k).start()
        small_copy(k).start()
        return 0

    lax.fori_loop(1, NCP, start, 0)
    mine = pltpu.make_async_copy(tiles.at[:, 0], got.at[me], own.at[0])
    mine.start()
    mine_small = pltpu.make_async_copy(small.at[0], got_small.at[me], own.at[1])
    mine_small.start()

    def pass_on(k, _):
        row_copy(k).wait_recv()
        forward(k).start()
        return 0

    lax.fori_loop(1, NCP, pass_on, 0)
    mine.wait()
    mine_small.wait()

    def finish(k, _):
        row_copy(k).wait_send()
        small_copy(k).wait()
        forward(k).wait()
        return 0

    lax.fori_loop(1, NCP, finish, 0)


def exchange(tiles, small):
    any_spec = pl.BlockSpec(memory_space=pl.ANY)
    return pl.pallas_call(
        exchange_kernel,
        out_shape=(
            jax.ShapeDtypeStruct((NCP, 16, 16, F), BF),
            jax.ShapeDtypeStruct((NCP, 16, SEG), BF),
        ),
        in_specs=[any_spec] * 2,
        out_specs=[any_spec] * 2,
        scratch_shapes=[pltpu.SemaphoreType.DMA((NCP,))] * 6 + [pltpu.SemaphoreType.DMA((2,))],
        compiler_params=pltpu.CompilerParams(collective_id=0, has_side_effects=True),
        name="exchange",
    )(tiles, small)


def double_cdf(u):
    far = TAIL[3]
    for coef in TAIL[2::-1]:
        far = far * u + coef
    return jnp.where(u < FAR, jnp.exp2(far), 1.0 + lax.erf(u))


def forward_kernel(lengths, got, got_small, factors, prob, loss, comp, shift, slope, expo, wide, expo_t):
    position = lax.axis_index("cp")

    @pl.when(pl.program_id(0) == 0)
    def _():
        comp[...] = jnp.zeros_like(comp)
        wide[...] = jnp.zeros_like(wide)
        index = lax.broadcasted_iota(jnp.int32, (SEG, 128), 0)
        lane = lax.broadcasted_iota(jnp.int32, (SEG, 128), 1)
        for block, (start, offset, live) in enumerate(spots(lengths, position)):
            at = pl.ds(pl.multiple_of(start * 16, 16), SEG)
            comp[at, :] = got[block]
            part = got_small[block].astype(F32)
            part = jnp.concatenate([part, jnp.zeros((112, SEG), F32)], axis=0).T
            row = (offset + 16 * (index // 16)) * 16 + index % 16
            keep = (row < live) | (lane >= 8)
            wide[at, :] = jnp.where(keep, part, 0.0)

        def scale(i, _):
            at = pl.ds(pl.multiple_of(i * 128, 128), 128)
            rows = comp[at, :].astype(F32)
            total = jnp.sum(rows * rows, axis=1, keepdims=True)
            by = lax.rsqrt(1.0 + total) * ROOT_HALF
            slope[at, :] = jnp.broadcast_to(by, (128, 128))
            part = wide[at, :]
            shift[at, :] = jnp.broadcast_to(part[:, 8:9] * by, (128, 128))
            expo[at, :] = part.astype(BF)
            expo_t[:, at] = part.T[0:16, :].astype(BF)
            return 0

        lax.fori_loop(0, CAP // 128, scale, 0)

    def chunk(i, _):
        at = pl.ds(pl.multiple_of(i * CHUNK, 16), CHUNK)
        project = lax.dot_general(
            comp[at, :], factors[...], (((1,), (1,)), ((), ())), preferred_element_type=F32
        )
        a = jnp.concatenate([shift[at, :]] * (ST // 128), axis=1)
        b = jnp.concatenate([slope[at, :]] * (ST // 128), axis=1)
        prob[at, :] = double_cdf(a - project * b).astype(BF)
        return 0

    lax.fori_loop(0, CAP // CHUNK, chunk, 0)
    loss[...] = jnp.dot(expo_t[...], prob[...], preferred_element_type=F32)[0:8, :]


def forward(lengths, got, got_small, factors):
    whole = lambda shape: pl.BlockSpec(shape, lambda i: (0,) * len(shape))
    return pl.pallas_call(
        forward_kernel,
        grid=(S // ST,),
        out_shape=(
            jax.ShapeDtypeStruct((CAP, S), BF),
            jax.ShapeDtypeStruct((8, S), F32),
            jax.ShapeDtypeStruct((CAP + SEG, F), BF),
            jax.ShapeDtypeStruct((CAP, 128), F32),
            jax.ShapeDtypeStruct((CAP, 128), F32),
            jax.ShapeDtypeStruct((CAP, 128), BF),
        ),
        in_specs=[
            pl.BlockSpec(memory_space=pltpu.SMEM),
            whole((NCP, SEG, F)),
            whole((NCP, 16, SEG)),
            pl.BlockSpec((ST, F), lambda i: (i, 0)),
        ],
        out_specs=[
            pl.BlockSpec((CAP, ST), lambda i: (0, i)),
            pl.BlockSpec((8, ST), lambda i: (0, i)),
            whole((CAP + SEG, F)),
            whole((CAP, 128)),
            whole((CAP, 128)),
            whole((CAP, 128)),
        ],
        scratch_shapes=[pltpu.VMEM((CAP + SEG, 128), F32), pltpu.VMEM((16, CAP), BF)],
        compiler_params=pltpu.CompilerParams(vmem_limit_bytes=48 * 2**20),
        name="forward",
    )(lengths, got, got_small, factors)


def softmax_kernel(loss, aversion, weights, risk, parts, mine, every, stats, sends, recvs, sends_g, recvs_g, sends_z, recvs_z):
    me = lax.axis_index("cp")
    sc = lax.axis_index("sc")
    width = S // NCP
    barrier = pltpu.get_barrier_semaphore()

    def greet(k, _):
        pl.semaphore_signal(barrier, inc=1, device_id=((me + k) % NCP, sc), device_id_type=MESH)
        return 0

    def greet_z(k, _):
        pl.semaphore_signal(barrier, inc=1, device_id=(me, (sc + k) % NSC), device_id_type=MESH)
        return 0

    lax.fori_loop(1, NCP, greet, 0)
    lax.fori_loop(1, NSC, greet_z, 0)
    pl.semaphore_wait(barrier, NCP + NSC - 2)

    def part_of(position):
        return pl.ds(pl.multiple_of(position * width, width), width)

    def scatter(k):
        peer = (me + k) % NCP
        return pltpu.make_async_remote_copy(
            src_ref=loss.at[:, part_of(peer)],
            dst_ref=parts.at[me],
            send_sem=sends.at[k],
            recv_sem=recvs.at[k],
            device_id=(peer, sc),
            device_id_type=MESH,
        )

    def gather(k):
        return pltpu.make_async_remote_copy(
            src_ref=mine,
            dst_ref=every.at[:, part_of(me)],
            send_sem=sends_g.at[k],
            recv_sem=recvs_g.at[k],
            device_id=((me + k) % NCP, sc),
            device_id_type=MESH,
        )

    def share(k):
        return pltpu.make_async_remote_copy(
            src_ref=stats.at[sc],
            dst_ref=stats.at[sc],
            send_sem=sends_z.at[k],
            recv_sem=recvs_z.at[k],
            device_id=(me, (sc + k) % NSC),
            device_id_type=MESH,
        )

    def run(count, act):
        def body(k, _):
            act(k)
            return 0

        lax.fori_loop(1, count, body, 0)

    run(NCP, lambda k: scatter(k).start())
    parts[me] = loss[:, part_of(me)]
    run(NCP, lambda k: scatter(k).wait_recv())
    total = parts[0]
    for i in range(1, NCP):
        total = total + parts[i]
    averse = aversion[...]
    averse_two = jnp.concatenate([averse] * (width // 128), axis=1)
    score = averse_two * (total * (0.5 / LIVE))
    mine[...] = score
    run(NCP, lambda k: gather(k).start())
    every[:, part_of(me)] = score
    run(NCP, lambda k: gather(k).wait_recv())
    scores = every[...]
    top = jnp.max(scores, axis=1, keepdims=True)
    raised = jnp.exp(scores - top)
    mass = jnp.sum(raised, axis=1, keepdims=True)
    stats[sc, 0:8, :] = jnp.broadcast_to(top, (8, 128))
    stats[sc, 8:16, :] = jnp.broadcast_to(mass, (8, 128))
    run(NSC, lambda k: share(k).start())
    run(NSC, lambda k: share(k).wait_recv())
    best = stats[0, 0:8, :]
    for i in range(1, NSC):
        best = jnp.maximum(best, stats[i, 0:8, :])
    heap = jnp.zeros((8, 128), F32)
    for i in range(NSC):
        heap = heap + stats[i, 8:16, :] * jnp.exp(stats[i, 0:8, :] - best)
    final = (jnp.exp(scores - best[:, 0:1]) / heap[:, 0:1]).astype(BF)
    weights[...] = jnp.concatenate([final.astype(F32), jnp.zeros((8, S), F32)], axis=0).astype(BF)
    risk[...] = (best + jnp.log(heap / SCEN)) / averse
    run(NCP, lambda k: scatter(k).wait_send())
    run(NCP, lambda k: gather(k).wait_send())
    run(NSC, lambda k: share(k).wait_send())


def softmax(loss, aversion):
    vmem = pl.BlockSpec(memory_space=pltpu.VMEM)
    dma = pltpu.SemaphoreType.DMA
    return pl.pallas_call(
        softmax_kernel,
        out_shape=(jax.ShapeDtypeStruct((16, S), BF), jax.ShapeDtypeStruct((8, 128), F32)),
        in_specs=[vmem] * 2,
        out_specs=[vmem] * 2,
        scratch_shapes=[
            pltpu.VMEM((NCP, 8, S // NCP), F32),
            pltpu.VMEM((8, S // NCP), F32),
            pltpu.VMEM((8, S), F32),
            pltpu.VMEM((NSC, 16, 128), F32),
            dma((NCP,)),
            dma((NCP,)),
            dma((NCP,)),
            dma((NCP,)),
            dma((NSC,)),
            dma((NSC,)),
        ],
        compiler_params=pltpu.CompilerParams(collective_id=1, has_side_effects=True),
        name="softmax",
    )(loss, aversion)


def backward_kernel(comp, shift, slope, expo, factors, weights, prob, out, load_acc, lat_acc, thr_acc, expo_acc, turned):
    step = pl.program_id(0)

    @pl.when(step == 0)
    def _():
        load_acc[...] = jnp.zeros_like(load_acc)
        lat_acc[...] = jnp.zeros_like(lat_acc)
        thr_acc[...] = jnp.zeros_like(thr_acc)
        expo_acc[...] = jnp.zeros_like(expo_acc)

    turned[:, 0:16] = weights[...].astype(F32).T.astype(BF)

    def chunk(i, _):
        at = pl.ds(pl.multiple_of(i * CHUNK, 16), CHUNK)
        project = lax.dot_general(
            comp[at, :], factors[...], (((1,), (1,)), ((), ())), preferred_element_type=F32
        )
        pull = jnp.dot(expo[at, 0:16], weights[...], preferred_element_type=F32)
        a = jnp.concatenate([shift[at, :]] * (ST // 128), axis=1)
        b = jnp.concatenate([slope[at, :]] * (ST // 128), axis=1)
        u = a - project * b
        heavy = pull * jnp.exp2(u * u * (-LOG2E))
        lat = heavy * u
        lat_sum = lat[:, 0:128]
        thr_sum = heavy[:, 0:128]
        for k in range(1, ST // 128):
            lat_sum = lat_sum + lat[:, k * 128 : (k + 1) * 128]
            thr_sum = thr_sum + heavy[:, k * 128 : (k + 1) * 128]
        lat_acc[at, :] += lat_sum
        thr_acc[at, :] += thr_sum
        load_acc[at, :] += jnp.dot(heavy.astype(BF), factors[...], preferred_element_type=F32)
        expo_acc[at, :] += jnp.dot(prob[at, :], turned[:, 0:16], preferred_element_type=F32)
        return 0

    lax.fori_loop(0, CAP // CHUNK, chunk, 0)

    @pl.when(step == pl.num_programs(0) - 1)
    def _():
        scale = 1.0 / (LIVE * math.sqrt(2.0 * math.pi))

        def fold(i, _):
            at = pl.ds(pl.multiple_of(i * 128, 128), 128)
            by = slope[at, 0:1] * math.sqrt(2.0)
            lat = jnp.sum(lat_acc[at, :], axis=1, keepdims=True) * (scale * math.sqrt(2.0))
            thr = jnp.sum(thr_acc[at, :], axis=1, keepdims=True) * scale * by
            rows = comp[at, :].astype(F32)
            grad = -(load_acc[at, :] * (scale * by)) - (lat * by * by) * rows
            flat = grad.T
            dates = jnp.concatenate([expo_acc[at, :], jnp.zeros((128, 112), F32)], axis=1).T
            dates = dates[0:8, :] * (0.5 / LIVE)
            limits = jnp.broadcast_to(thr, (128, 128)).T
            for j in range(NSC):
                out[j, 0:32, at] = flat[32 * j : 32 * (j + 1), :]
                out[j, 32:40, at] = jnp.concatenate(
                    [dates[j : j + 1, :], limits[0:7, :]], axis=0
                )
            return 0

        lax.fori_loop(0, CAP // 128, fold, 0)


def backward(comp, shift, slope, expo, factors, weights, prob):
    whole = lambda shape: pl.BlockSpec(shape, lambda i: (0,) * len(shape))
    return pl.pallas_call(
        backward_kernel,
        grid=(S // ST,),
        out_shape=jax.ShapeDtypeStruct((NSC, 40, CAP), F32),
        in_specs=[
            whole((CAP + SEG, F)),
            whole((CAP, 128)),
            whole((CAP, 128)),
            whole((CAP, 128)),
            pl.BlockSpec((ST, F), lambda i: (i, 0)),
            pl.BlockSpec((16, ST), lambda i: (0, i)),
            pl.BlockSpec((CAP, ST), lambda i: (0, i)),
        ],
        out_specs=whole((NSC, 40, CAP)),
        scratch_shapes=[
            pltpu.VMEM((CAP, F), F32),
            pltpu.VMEM((CAP, 128), F32),
            pltpu.VMEM((CAP, 128), F32),
            pltpu.VMEM((CAP, 16), F32),
            pltpu.VMEM((ST, 128), BF),
        ],
        compiler_params=pltpu.CompilerParams(vmem_limit_bytes=48 * 2**20),
        name="backward",
    )(comp, shift, slope, expo, factors, weights, prob)


def run(first, last, act):
    def body(k, _):
        act(k)
        return 0

    lax.fori_loop(first, last, body, 0)


def add_kernel(grads, full, pair, sum_l, sum_s, near_l, near_s, sends_a, recvs_a, sends_b, recvs_b):
    me = lax.axis_index("cp")
    sc = lax.axis_index("sc")
    core = sc % 2
    z = sc // 2
    sibling = sc + 1 - 2 * core
    barrier = pltpu.get_barrier_semaphore()
    pl.semaphore_signal(barrier, inc=1, device_id=(me, sibling), device_id_type=MESH)
    run(1, 4, lambda k: pl.semaphore_signal(barrier, inc=1, device_id=(me, ((z + k) % 4) * 2 + core), device_id_type=MESH))
    pl.semaphore_wait(barrier, 4)

    def pair_copy(k):
        to = (z + k) % 4
        return pltpu.make_async_remote_copy(
            src_ref=grads.at[to * 2 + 1 - core],
            dst_ref=pair.at[k],
            send_sem=sends_a.at[k],
            recv_sem=recvs_a.at[k],
            device_id=(me, sibling),
            device_id_type=MESH,
        )

    def near_copy(k, which):
        src, dst = ((sum_l, near_l), (sum_s, near_s))[which]
        return pltpu.make_async_remote_copy(
            src_ref=src.at[k],
            dst_ref=dst.at[k],
            send_sem=sends_b.at[which, k],
            recv_sem=recvs_b.at[which, k],
            device_id=(me, ((z + k) % 4) * 2 + core),
            device_id_type=MESH,
        )

    for k in (2, 1, 3, 0):
        pair_copy(k).start()
    for k in (2, 1, 3):
        pair_copy(k).wait_recv()
        share = ((z + k) % 4) * 2 + core
        sum_l[k] = (grads[share, 0:32, :] + pair[k, 0:32, :]).astype(BF)
        sum_s[k] = grads[share, 32:40, :] + pair[k, 32:40, :]
        near_copy(k, 0).start()
        near_copy(k, 1).start()
    pair_copy(0).wait_recv()
    full[:, 0:CAP] = grads[sc] + pair[0]
    for k in (1, 3, 2):
        near_copy(k, 0).wait_recv()
        near_copy(k, 1).wait_recv()
        full[0:32, 0:CAP] += near_l[k].astype(F32)
        full[32:40, 0:CAP] += near_s[k]
    full[:, CAP:] = jnp.zeros((40, 384), F32)
    for k in (0, 1, 2, 3):
        pair_copy(k).wait_send()
        if k:
            near_copy(k, 0).wait_send()
            near_copy(k, 1).wait_send()


def add_up(grads):
    vmem = pl.BlockSpec(memory_space=pltpu.VMEM)
    dma = pltpu.SemaphoreType.DMA
    return pl.pallas_call(
        add_kernel,
        out_shape=jax.ShapeDtypeStruct((40, CAP + 384), F32),
        in_specs=[vmem],
        out_specs=vmem,
        scratch_shapes=[
            pltpu.VMEM((4, 40, CAP), F32),
            pltpu.VMEM((4, 32, CAP), BF),
            pltpu.VMEM((4, 8, CAP), F32),
            pltpu.VMEM((4, 32, CAP), BF),
            pltpu.VMEM((4, 8, CAP), F32),
            dma((4,)),
            dma((4,)),
            dma((2, 4)),
            dma((2, 4)),
        ],
        compiler_params=pltpu.CompilerParams(
            collective_id=2, has_side_effects=True, vmem_limit_bytes=32 * 2**20
        ),
        name="add_up",
    )(grads)


def place_kernel(lengths, full, pack_l, pack_s):
    lane = lax.broadcasted_iota(jnp.int32, (40, SEG), 1)
    for block, (start, offset, live) in enumerate(spots(lengths, lax.axis_index("cp"))):
        at = pl.ds(pl.multiple_of((start // 8) * 128, 128), 384)
        piece = pltpu.roll(full[:, at], (24 - start % 8) * 16 % 384, 1)[:, 0:SEG]
        row = (offset + 16 * (lane // 16)) * 16 + lane % 16
        piece = jnp.where(row < live, piece, 0.0)
        pack_l[block] = piece[0:32, :].astype(BF)
        pack_s[block] = piece[32:40, :]


def place(lengths, full):
    vmem = pl.BlockSpec(memory_space=pltpu.VMEM)
    return pl.pallas_call(
        place_kernel,
        out_shape=(
            jax.ShapeDtypeStruct((NCP, 32, SEG), BF),
            jax.ShapeDtypeStruct((NCP, 8, SEG), F32),
        ),
        in_specs=[pl.BlockSpec(memory_space=pltpu.SMEM), vmem],
        out_specs=[vmem] * 2,
        name="place",
    )(lengths, full)


def return_kernel(
    pack_l, pack_s, load_out, thr_out, expo_out,
    back_l, back_s, line, sends_c, recvs_c, sends_d, recvs_d,
):
    me = lax.axis_index("cp")
    sc = lax.axis_index("sc")
    barrier = pltpu.get_barrier_semaphore()
    run(1, NCP, lambda k: pl.semaphore_signal(barrier, inc=1, device_id=((me + k) % NCP, sc), device_id_type=MESH))
    run(1, NSC, lambda k: pl.semaphore_signal(barrier, inc=1, device_id=(me, (sc + k) % NSC), device_id_type=MESH))
    pl.semaphore_wait(barrier, NCP + NSC - 2)

    def back_copy(k, which):
        src, dst = ((pack_l, back_l), (pack_s, back_s))[which]
        peer = (me + k) % NCP
        return pltpu.make_async_remote_copy(
            src_ref=src.at[peer],
            dst_ref=dst.at[(me - peer + NCP) % NCP],
            send_sem=sends_c.at[which, k],
            recv_sem=recvs_c.at[which, k],
            device_id=(peer, sc),
            device_id_type=MESH,
        )

    run(1, NCP, lambda k: (back_copy(k, 0).start(), back_copy(k, 1).start()))
    back_l[0] = pack_l[me]
    back_s[0] = pack_s[me]
    run(1, NCP, lambda k: (back_copy(k, 0).wait_recv(), back_copy(k, 1).wait_recv()))

    group = lax.broadcasted_iota(jnp.int32, (40, 128), 1) // 16
    for g in range(2):
        for h in range(2):
            held = [
                jnp.concatenate(
                    [
                        back_l[8 * g + q, :, 128 * h : 128 * (h + 1)].astype(F32),
                        back_s[8 * g + q, :, 128 * h : 128 * (h + 1)],
                    ],
                    axis=0,
                )
                for q in range(8)
            ]
            for s in range(8):
                mixed = held[s]
                for q in range(8):
                    if q != s:
                        mixed = jnp.where(group == q, pltpu.roll(held[q], (16 * (q - s)) % 128, 1), mixed)
                    elif s > 0:
                        pass
                tile = 2 * (8 * h + s) + g
                load_out[:, 128 * tile : 128 * (tile + 1)] = mixed[0:32, :]
                line[0:1, 128 * tile : 128 * (tile + 1)] = mixed[32:33, :]
                thr_out[:, 128 * tile : 128 * (tile + 1)] = mixed[33:34, :]

    expo_out[sc] = line[...]

    def date_copy(k):
        return pltpu.make_async_remote_copy(
            src_ref=line,
            dst_ref=expo_out.at[sc],
            send_sem=sends_d.at[k],
            recv_sem=recvs_d.at[k],
            device_id=(me, (sc + k) % NSC),
            device_id_type=MESH,
        )

    run(1, NSC, lambda k: date_copy(k).start())
    run(1, NSC, lambda k: date_copy(k).wait())
    run(1, NCP, lambda k: (back_copy(k, 0).wait_send(), back_copy(k, 1).wait_send()))


def give_back(pack_l, pack_s):
    vmem = pl.BlockSpec(memory_space=pltpu.VMEM)
    dma = pltpu.SemaphoreType.DMA
    return pl.pallas_call(
        return_kernel,
        out_shape=(
            jax.ShapeDtypeStruct((32, ROWS), F32),
            jax.ShapeDtypeStruct((1, ROWS), F32),
            jax.ShapeDtypeStruct((NSC, 1, ROWS), F32),
        ),
        in_specs=[vmem] * 2,
        out_specs=[vmem] * 3,
        scratch_shapes=[
            pltpu.VMEM((NCP, 32, SEG), BF),
            pltpu.VMEM((NCP, 8, SEG), F32),
            pltpu.VMEM((1, ROWS), F32),
            dma((2, NCP)),
            dma((2, NCP)),
            dma((NSC,)),
            dma((NSC,)),
        ],
        compiler_params=pltpu.CompilerParams(collective_id=3, has_side_effects=True),
        name="give_back",
    )(pack_l, pack_s)


def per_device(factors, loadings, thresholds, exposures, aversion, lengths):
    tiles = loadings.reshape(16, NCP, 16, F)
    small = jnp.concatenate(
        [exposures.T, thresholds[None, :], jnp.zeros((7, ROWS), BF)], axis=0
    )
    small = small.reshape(16, 16, NCP, 16).transpose(2, 0, 1, 3).reshape(NCP, 16, SEG)
    got, got_small = exchange(tiles, small)
    prob, loss, comp, shift, slope, expo = forward(
        lengths, got.reshape(NCP, SEG, F), got_small, factors
    )
    weights, risk = softmax(loss, jnp.broadcast_to(aversion[:, None], (8, 128)))
    grads = backward(comp, shift, slope, expo, factors, weights, prob)
    load, thr, dates = give_back(*place(lengths, add_up(grads)))
    return (load.T, thr.reshape(ROWS), dates.reshape(NSC, ROWS).T, risk[:, 0])


def solution(mesh):
    in_specs = (P("sc", None), P("cp", None), P("cp"), P("cp", None), P(), P())
    out_specs = (P("cp", "sc"), P("cp"), P("cp", None), P())
    return jax.shard_map(
        per_device, mesh=mesh, in_specs=in_specs, out_specs=out_specs, check_vma=False
    )
```

```python
import math

import jax
import jax.numpy as jnp
from jax import lax
from jax.experimental import pallas as pl
from jax.experimental.pallas import tpu as pltpu
from jax.sharding import PartitionSpec as P

MESH = pl.DeviceIdType.MESH
NCP = 16
NSC = 8
F = 256
ROWS = 4096
S = 4096
CAP = 2176
SEG = ROWS // NCP
LIVE = 32768
SCEN = 32768
ST = 512
CHUNKS = ((0, 768), (768, 768), (1536, 640))
ROOT_HALF = 0.7071067811865476
LOG2E = 1.4426950408889634
FAR = -3.1
TAIL = (-0.750217616, 0.756257034, -1.37553279, 0.0025935648)
BF = jnp.bfloat16
F32 = jnp.float32


def spots(lengths_ref, position):
    start = jnp.int32(0)
    out = []
    for block in range(NCP):
        live = lengths_ref[block]
        tiles = (live + 15) // 16
        offset = (position - block + NCP) % NCP
        out.append((start, offset, live))
        start = start + (tiles - offset + 15) // 16
    return out


def exchange_kernel(tiles, small, got, got_small, sends, recvs, sends_s, recvs_s, sends_b, recvs_b, own):
    me = lax.axis_index("cp")
    sc = lax.axis_index("sc")
    core = sc % 2
    sibling = sc + 1 - 2 * core
    barrier = pltpu.get_barrier_semaphore()

    def greet(k, _):
        pl.semaphore_signal(barrier, inc=1, device_id=((me + k) % NCP, sc), device_id_type=MESH)
        return 0

    lax.fori_loop(1, NCP, greet, 0)
    pl.semaphore_signal(barrier, inc=1, device_id=(me, sibling), device_id_type=MESH)
    pl.semaphore_wait(barrier, NCP)

    half = pl.ds(core * 8, 8)

    def row_copy(k):
        peer = (me + k) % NCP
        return pltpu.make_async_remote_copy(
            src_ref=tiles.at[half, (peer - me + NCP) % NCP],
            dst_ref=got.at[me, half],
            send_sem=sends.at[k],
            recv_sem=recvs.at[k],
            device_id=(peer, sc),
            device_id_type=MESH,
        )

    def small_copy(k):
        peer = (me + k) % NCP
        return pltpu.make_async_remote_copy(
            src_ref=small.at[(peer - me + NCP) % NCP],
            dst_ref=got_small.at[me],
            send_sem=sends_s.at[k],
            recv_sem=recvs_s.at[k],
            device_id=(peer, sc),
            device_id_type=MESH,
        )

    def forward(k):
        source = (me - k + NCP) % NCP
        return pltpu.make_async_remote_copy(
            src_ref=got.at[source, half],
            dst_ref=got.at[source, half],
            send_sem=sends_b.at[k],
            recv_sem=recvs_b.at[k],
            device_id=(me, sibling),
            device_id_type=MESH,
        )

    def start(k, _):
        row_copy(k).start()
        small_copy(k).start()
        return 0

    lax.fori_loop(1, NCP, start, 0)
    mine = pltpu.make_async_copy(tiles.at[:, 0], got.at[me], own.at[0])
    mine.start()
    mine_small = pltpu.make_async_copy(small.at[0], got_small.at[me], own.at[1])
    mine_small.start()

    def pass_on(k, _):
        row_copy(k).wait_recv()
        forward(k).start()
        return 0

    lax.fori_loop(1, NCP, pass_on, 0)
    mine.wait()
    mine_small.wait()

    def finish(k, _):
        row_copy(k).wait_send()
        small_copy(k).wait()
        forward(k).wait()
        return 0

    lax.fori_loop(1, NCP, finish, 0)


def exchange(tiles, small):
    any_spec = pl.BlockSpec(memory_space=pl.ANY)
    return pl.pallas_call(
        exchange_kernel,
        out_shape=(
            jax.ShapeDtypeStruct((NCP, 16, 16, F), BF),
            jax.ShapeDtypeStruct((NCP, 16, SEG), BF),
        ),
        in_specs=[any_spec] * 2,
        out_specs=[any_spec] * 2,
        scratch_shapes=[pltpu.SemaphoreType.DMA((NCP,))] * 6 + [pltpu.SemaphoreType.DMA((2,))],
        compiler_params=pltpu.CompilerParams(collective_id=0, has_side_effects=True),
        name="exchange",
    )(tiles, small)


def double_cdf(u):
    far = TAIL[3]
    for coef in TAIL[2::-1]:
        far = far * u + coef
    return jnp.where(u < FAR, jnp.exp2(far), 1.0 + lax.erf(u))


def run(first, last, act):
    def body(k, _):
        act(k)
        return 0

    lax.fori_loop(first, last, body, 0)


def compact_kernel(lengths, got, got_small, comp, shift, slope, expo, expo_t, wide):
    comp[...] = jnp.zeros_like(comp)
    wide[...] = jnp.zeros_like(wide)
    index = lax.broadcasted_iota(jnp.int32, (SEG, 128), 0)
    lane = lax.broadcasted_iota(jnp.int32, (SEG, 128), 1)
    for block, (start, offset, live) in enumerate(spots(lengths, lax.axis_index("cp"))):
        at = pl.ds(pl.multiple_of(start * 16, 16), SEG)
        comp[at, :] = got[block]
        part = got_small[block].astype(F32)
        part = jnp.concatenate([part, jnp.zeros((112, SEG), F32)], axis=0).T
        row = (offset + 16 * (index // 16)) * 16 + index % 16
        keep = (row < live) | (lane >= 8)
        wide[at, :] = jnp.where(keep, part, 0.0)

    def scale(i, _):
        at = pl.ds(pl.multiple_of(i * 128, 128), 128)
        rows = comp[at, :].astype(F32)
        total = jnp.sum(rows * rows, axis=1, keepdims=True)
        by = lax.rsqrt(1.0 + total) * ROOT_HALF
        slope[at, :] = jnp.broadcast_to(by, (128, 128))
        part = wide[at, :]
        shift[at, :] = jnp.broadcast_to(part[:, 8:9] * by, (128, 128))
        expo[at, :] = part.astype(BF)
        expo_t[:, at] = part.T[0:16, :].astype(BF)
        return 0

    lax.fori_loop(0, CAP // 128, scale, 0)


def compact(lengths, got, got_small):
    vmem = pl.BlockSpec(memory_space=pltpu.VMEM)
    return pl.pallas_call(
        compact_kernel,
        out_shape=(
            jax.ShapeDtypeStruct((CAP + SEG, F), BF),
            jax.ShapeDtypeStruct((CAP, 128), F32),
            jax.ShapeDtypeStruct((CAP, 128), F32),
            jax.ShapeDtypeStruct((CAP, 128), BF),
            jax.ShapeDtypeStruct((16, CAP), BF),
        ),
        in_specs=[pl.BlockSpec(memory_space=pltpu.SMEM), vmem, vmem],
        out_specs=[vmem] * 5,
        scratch_shapes=[pltpu.VMEM((CAP + SEG, 128), F32)],
        name="compact",
    )(lengths, got, got_small)


def main_kernel(
    comp, shift, slope, expo, expo_t, factors, aversion, full, risk,
    prob, loss, parts, mine, every, stats, weights, turned,
    expo_acc, dates, dates_in, date_sum, date_all,
    load_acc, lat_acc, thr_acc, grads, pair, sum_l, near_l, thr_line, thr_pair, thr_sum, thr_near,
    sends, recvs, sends_g, recvs_g, sends_z, recvs_z, sends_d, recvs_d, sends_e, recvs_e,
    sends_a, recvs_a, sends_b, recvs_b, sends_t, recvs_t,
):
    me = lax.axis_index("cp")
    sc = lax.axis_index("sc")
    core = sc % 2
    z = sc // 2
    sibling = sc + 1 - 2 * core
    width = S // NCP
    barrier = pltpu.get_barrier_semaphore()
    run(1, NCP, lambda k: pl.semaphore_signal(barrier, inc=1, device_id=((me + k) % NCP, sc), device_id_type=MESH))
    run(1, NSC, lambda k: pl.semaphore_signal(barrier, inc=1, device_id=(me, (sc + k) % NSC), device_id_type=MESH))

    def remote(src, dst, send, recv, to):
        return pltpu.make_async_remote_copy(
            src_ref=src, dst_ref=dst, send_sem=send, recv_sem=recv, device_id=to, device_id_type=MESH
        )

    def latent(first, count, cols):
        rows = pl.ds(first, count)
        project = lax.dot_general(
            comp[rows, :], factors[cols, :], (((1,), (1,)), ((), ())), preferred_element_type=F32
        )
        a = jnp.concatenate([shift[rows, :]] * (ST // 128), axis=1)
        b = jnp.concatenate([slope[rows, :]] * (ST // 128), axis=1)
        return a - project * b

    def ahead(step):
        cols = pl.ds(pl.multiple_of(step * ST, ST), ST)
        for first, count in CHUNKS:
            prob[pl.ds(first, count), cols] = double_cdf(latent(first, count, cols)).astype(BF)
        loss[:, cols] = jnp.dot(expo_t[...], prob[:, cols], preferred_element_type=F32)[0:8, :]

    run(0, S // ST, ahead)
    pl.semaphore_wait(barrier, NCP + NSC - 2)

    def part_of(position):
        return pl.ds(pl.multiple_of(position * width, width), width)

    def scatter(k):
        peer = (me + k) % NCP
        return remote(loss.at[:, part_of(peer)], parts.at[me], sends.at[k], recvs.at[k], (peer, sc))

    def gather(k):
        return remote(mine, every.at[:, part_of(me)], sends_g.at[k], recvs_g.at[k], ((me + k) % NCP, sc))

    def share(k):
        return remote(stats.at[sc], stats.at[sc], sends_z.at[k], recvs_z.at[k], (me, (sc + k) % NSC))

    run(1, NCP, lambda k: scatter(k).start())
    parts[me] = loss[:, part_of(me)]
    at_date = lax.broadcasted_iota(jnp.int32, (8, 128), 0)
    averse = jnp.zeros((8, 128), F32)
    for t in range(8):
        averse = jnp.where(at_date == t, aversion[t], averse)
    run(1, NCP, lambda k: scatter(k).wait_recv())
    total = parts[0]
    for i in range(1, NCP):
        total = total + parts[i]
    score = jnp.concatenate([averse] * (width // 128), axis=1) * (total * (0.5 / LIVE))
    mine[...] = score
    run(1, NCP, lambda k: gather(k).start())
    every[:, part_of(me)] = score
    run(1, NCP, lambda k: gather(k).wait_recv())
    scores = every[...]
    top = jnp.max(scores, axis=1, keepdims=True)
    mass = jnp.sum(jnp.exp(scores - top), axis=1, keepdims=True)
    stats[sc, 0:8, :] = jnp.broadcast_to(top, (8, 128))
    stats[sc, 8:16, :] = jnp.broadcast_to(mass, (8, 128))
    run(1, NSC, lambda k: share(k).start())
    run(1, NSC, lambda k: share(k).wait_recv())
    best = stats[0, 0:8, :]
    for i in range(1, NSC):
        best = jnp.maximum(best, stats[i, 0:8, :])
    heap = jnp.zeros((8, 128), F32)
    for i in range(NSC):
        heap = heap + stats[i, 8:16, :] * jnp.exp(stats[i, 0:8, :] - best)
    final = jnp.exp(every[...] - best[:, 0:1]) / heap[:, 0:1]
    weights[...] = jnp.concatenate([final, jnp.zeros((8, S), F32)], axis=0).astype(BF)
    risk[...] = (best + jnp.log(heap / SCEN)) / averse
    run(1, NCP, lambda k: scatter(k).wait_send())
    run(1, NCP, lambda k: gather(k).wait_send())
    run(1, NSC, lambda k: share(k).wait_send())

    expo_acc[...] = jnp.zeros_like(expo_acc)

    def expose(step):
        cols = pl.ds(pl.multiple_of(step * ST, ST), ST)
        turned[:, 0:16] = weights[:, cols].astype(F32).T.astype(BF)
        expo_acc[...] += jnp.dot(prob[:, cols], turned[:, 0:16], preferred_element_type=F32)

    run(0, S // ST, expose)
    for i in range(CAP // 128):
        block = jnp.concatenate(
            [expo_acc[128 * i : 128 * (i + 1), :], jnp.zeros((128, 112), F32)], axis=1
        ).T
        for j in range(NSC):
            dates[j, :, 128 * i : 128 * (i + 1)] = block[j : j + 1, :] * (0.5 / LIVE)

    def date_out(k):
        peer = (sc + k) % NSC
        return remote(dates.at[peer], dates_in.at[k], sends_d.at[k], recvs_d.at[k], (me, peer))

    def date_share(k):
        return remote(date_sum, date_all.at[sc], sends_e.at[k], recvs_e.at[k], (me, (sc + k) % NSC))

    run(1, NSC, lambda k: date_out(k).start())

    def pair_copy(c, k):
        first, count = CHUNKS[c]
        at = pl.ds(first, count)
        return remote(
            grads.at[((z + k) % 4) * 2 + 1 - core, :, at], pair.at[k, :, at],
            sends_a.at[c, k], recvs_a.at[c, k], (me, sibling),
        )

    def thr_pair_copy(c):
        at = pl.ds(*CHUNKS[c])
        return remote(thr_line.at[:, at], thr_pair.at[:, at], sends_a.at[c, 4], recvs_a.at[c, 4], (me, sibling))

    def near_copy(c, k):
        at = pl.ds(*CHUNKS[c])
        return remote(
            sum_l.at[k, :, at], near_l.at[k, :, at],
            sends_b.at[c, k], recvs_b.at[c, k], (me, ((z + k) % 4) * 2 + core),
        )

    def thr_near_copy(c, k):
        at = pl.ds(*CHUNKS[c])
        return remote(
            thr_sum.at[:, at], thr_near.at[k, :, at],
            sends_t.at[c, k], recvs_t.at[c, k], (me, ((z + k) % 4) * 2 + core),
        )

    def back_steps(c, low, high):
        first, count = CHUNKS[c]
        rows = pl.ds(first, count)
        acc = pl.ds(0, count)

        def step(i):
            cols = pl.ds(pl.multiple_of(i * ST, ST), ST)
            pull = jnp.dot(expo[rows, 0:16], weights[:, cols], preferred_element_type=F32)
            u = latent(first, count, cols)
            heavy = pull * jnp.exp2(u * u * (-LOG2E))
            lat = heavy * u
            lat_sum = lat[:, 0:128]
            thr_part = heavy[:, 0:128]
            for k in range(1, ST // 128):
                lat_sum = lat_sum + lat[:, k * 128 : (k + 1) * 128]
                thr_part = thr_part + heavy[:, k * 128 : (k + 1) * 128]
            lat_acc[acc, :] += lat_sum
            thr_acc[acc, :] += thr_part
            load_acc[acc, :] += jnp.dot(heavy.astype(BF), factors[cols, :], preferred_element_type=F32)

        run(low, high, step)

    def fold(c):
        first, count = CHUNKS[c]
        scale = 1.0 / (LIVE * math.sqrt(2.0 * math.pi))

        def one(i):
            rows = pl.ds(pl.multiple_of(first + i * 128, 128), 128)
            acc = pl.ds(pl.multiple_of(i * 128, 128), 128)
            by = slope[rows, 0:1] * math.sqrt(2.0)
            lat = jnp.sum(lat_acc[acc, :], axis=1, keepdims=True) * (scale * math.sqrt(2.0))
            thr = jnp.sum(thr_acc[acc, :], axis=1, keepdims=True) * scale * by
            grad = -(load_acc[acc, :] * (scale * by)) - (lat * by * by) * comp[rows, :].astype(F32)
            flat = grad.T
            for j in range(NSC):
                grads[j, :, rows] = flat[32 * j : 32 * (j + 1), :]
            thr_line[:, rows] = jnp.broadcast_to(thr, (128, 128)).T[0:1, :]

        run(0, count // 128, one)
        for k in (2, 1, 3, 0):
            pair_copy(c, k).start()
        thr_pair_copy(c).start()

    def pair_up(c):
        first, count = CHUNKS[c]
        at = pl.ds(first, count)
        for k in (2, 1, 3):
            pair_copy(c, k).wait_recv()
            sum_l[k, :, at] = (grads[((z + k) % 4) * 2 + core, :, at] + pair[k, :, at]).astype(BF)
            near_copy(c, k).start()
        thr_pair_copy(c).wait_recv()
        thr_sum[:, at] = thr_line[:, at] + thr_pair[:, at]
        for k in (2, 1, 3):
            thr_near_copy(c, k).start()
        pair_copy(c, 0).wait_recv()

    def near_up(c):
        first, count = CHUNKS[c]
        at = pl.ds(first, count)
        held = grads[sc, :, at] + pair[0, :, at]
        thr = thr_sum[:, at]
        for k in (1, 3, 2):
            near_copy(c, k).wait_recv()
            thr_near_copy(c, k).wait_recv()
            held = held + near_l[k, :, at].astype(F32)
            thr = thr + thr_near[k, :, at]
        full[0:32, at] = held
        full[40:41, at] = thr

    full[:, CAP:] = jnp.zeros((48, 384), F32)
    full[41:48, 0:CAP] = jnp.zeros((7, CAP), F32)
    steps = S // ST
    for c in range(len(CHUNKS)):
        load_acc[...] = jnp.zeros_like(load_acc)
        lat_acc[...] = jnp.zeros_like(lat_acc)
        thr_acc[...] = jnp.zeros_like(thr_acc)
        back_steps(c, 0, steps // 2)
        if c == 0:
            run(1, NSC, lambda k: date_out(k).wait_recv())
            line = dates[sc]
            for k in range(1, NSC):
                line = line + dates_in[k]
            date_sum[...] = line
            run(1, NSC, lambda k: date_share(k).start())
            date_all[sc] = line
        else:
            pair_up(c - 1)
        back_steps(c, steps // 2, steps)
        if c:
            near_up(c - 1)
        fold(c)
    last = len(CHUNKS) - 1
    run(1, NSC, lambda k: date_share(k).wait_recv())
    for j in range(NSC):
        full[32 + j : 33 + j, 0:CAP] = date_all[j]
    pair_up(last)
    run(1, NSC, lambda k: (date_out(k).wait_send(), date_share(k).wait_send()))
    near_up(last)
    for c in range(len(CHUNKS)):
        for k in range(4):
            pair_copy(c, k).wait_send()
        thr_pair_copy(c).wait_send()
        for k in range(1, 4):
            near_copy(c, k).wait_send()
            thr_near_copy(c, k).wait_send()


def main(comp, shift, slope, expo, expo_t, factors, aversion):
    vmem = pl.BlockSpec(memory_space=pltpu.VMEM)
    dma = pltpu.SemaphoreType.DMA
    parts = len(CHUNKS)
    most = max(count for _, count in CHUNKS)
    return pl.pallas_call(
        main_kernel,
        out_shape=(
            jax.ShapeDtypeStruct((48, CAP + 384), F32),
            jax.ShapeDtypeStruct((8, 128), F32),
        ),
        in_specs=[vmem] * 6 + [pl.BlockSpec(memory_space=pltpu.SMEM)],
        out_specs=[vmem] * 2,
        scratch_shapes=[
            pltpu.VMEM((CAP, S), BF),
            pltpu.VMEM((8, S), F32),
            pltpu.VMEM((NCP, 8, S // NCP), F32),
            pltpu.VMEM((8, S // NCP), F32),
            pltpu.VMEM((8, S), F32),
            pltpu.VMEM((NSC, 16, 128), F32),
            pltpu.VMEM((16, S), BF),
            pltpu.VMEM((ST, 128), BF),
            pltpu.VMEM((CAP, 16), F32),
            pltpu.VMEM((NSC, 1, CAP), F32),
            pltpu.VMEM((NSC, 1, CAP), F32),
            pltpu.VMEM((1, CAP), F32),
            pltpu.VMEM((NSC, 1, CAP), F32),
            pltpu.VMEM((most, F), F32),
            pltpu.VMEM((most, 128), F32),
            pltpu.VMEM((most, 128), F32),
            pltpu.VMEM((NSC, 32, CAP), F32),
            pltpu.VMEM((4, 32, CAP), F32),
            pltpu.VMEM((4, 32, CAP), BF),
            pltpu.VMEM((4, 32, CAP), BF),
            pltpu.VMEM((1, CAP), F32),
            pltpu.VMEM((1, CAP), F32),
            pltpu.VMEM((1, CAP), F32),
            pltpu.VMEM((4, 1, CAP), F32),
            dma((NCP,)),
            dma((NCP,)),
            dma((NCP,)),
            dma((NCP,)),
            dma((NSC,)),
            dma((NSC,)),
            dma((NSC,)),
            dma((NSC,)),
            dma((NSC,)),
            dma((NSC,)),
            dma((parts, 5)),
            dma((parts, 5)),
            dma((parts, 4)),
            dma((parts, 4)),
            dma((parts, 4)),
            dma((parts, 4)),
        ],
        compiler_params=pltpu.CompilerParams(
            collective_id=1, has_side_effects=True, vmem_limit_bytes=58 * 2**20
        ),
        name="main",
    )(comp, shift, slope, expo, expo_t, factors, aversion)


def place_kernel(lengths, full, pack):
    lane = lax.broadcasted_iota(jnp.int32, (48, SEG), 1)
    for block, (start, offset, live) in enumerate(spots(lengths, lax.axis_index("cp"))):
        at = pl.ds(pl.multiple_of((start // 8) * 128, 128), 384)
        piece = pltpu.roll(full[:, at], (24 - start % 8) * 16 % 384, 1)[:, 0:SEG]
        row = (offset + 16 * (lane // 16)) * 16 + lane % 16
        pack[block] = jnp.where(row < live, piece, 0.0).astype(BF)


def place(lengths, full):
    vmem = pl.BlockSpec(memory_space=pltpu.VMEM)
    return pl.pallas_call(
        place_kernel,
        out_shape=jax.ShapeDtypeStruct((NCP, 48, SEG), BF),
        in_specs=[pl.BlockSpec(memory_space=pltpu.SMEM), vmem],
        out_specs=vmem,
        name="place",
    )(lengths, full)


def return_kernel(pack, load_out, thr_out, expo_out, back, sends, recvs):
    me = lax.axis_index("cp")
    sc = lax.axis_index("sc")
    barrier = pltpu.get_barrier_semaphore()
    run(1, NCP, lambda k: pl.semaphore_signal(barrier, inc=1, device_id=((me + k) % NCP, sc), device_id_type=MESH))
    pl.semaphore_wait(barrier, NCP - 1)

    def back_copy(k):
        peer = (me + k) % NCP
        return pltpu.make_async_remote_copy(
            src_ref=pack.at[peer],
            dst_ref=back.at[(me - peer + NCP) % NCP],
            send_sem=sends.at[k],
            recv_sem=recvs.at[k],
            device_id=(peer, sc),
            device_id_type=MESH,
        )

    run(1, NCP, lambda k: back_copy(k).start())
    back[0] = pack[me]
    run(1, NCP, lambda k: back_copy(k).wait_recv())
    group = lax.broadcasted_iota(jnp.int32, (48, 128), 1) // 16
    for g in range(2):
        for h in range(2):
            held = [back[8 * g + q, :, 128 * h : 128 * (h + 1)].astype(F32) for q in range(8)]
            for s in range(8):
                mixed = held[s]
                for q in range(8):
                    if q != s:
                        turned = pltpu.roll(held[q], (16 * (q - s)) % 128, 1)
                        mixed = jnp.where(group == q, turned, mixed)
                tile = 2 * (8 * h + s) + g
                at = slice(128 * tile, 128 * (tile + 1))
                load_out[:, at] = mixed[0:32, :]
                expo_out[:, at] = mixed[32:40, :]
                thr_out[:, at] = mixed[40:41, :]
    run(1, NCP, lambda k: back_copy(k).wait_send())


def give_back(pack):
    vmem = pl.BlockSpec(memory_space=pltpu.VMEM)
    return pl.pallas_call(
        return_kernel,
        out_shape=(
            jax.ShapeDtypeStruct((32, ROWS), F32),
            jax.ShapeDtypeStruct((1, ROWS), F32),
            jax.ShapeDtypeStruct((NSC, ROWS), F32),
        ),
        in_specs=[vmem],
        out_specs=[vmem] * 3,
        scratch_shapes=[
            pltpu.VMEM((NCP, 48, SEG), BF),
            pltpu.SemaphoreType.DMA((NCP,)),
            pltpu.SemaphoreType.DMA((NCP,)),
        ],
        compiler_params=pltpu.CompilerParams(collective_id=2, has_side_effects=True),
        name="give_back",
    )(pack)


def per_device(factors, loadings, thresholds, exposures, aversion, lengths):
    tiles = loadings.reshape(16, NCP, 16, F)
    small = jnp.concatenate(
        [exposures.T, thresholds[None, :], jnp.zeros((7, ROWS), BF)], axis=0
    )
    small = small.reshape(16, 16, NCP, 16).transpose(2, 0, 1, 3).reshape(NCP, 16, SEG)
    got, got_small = exchange(tiles, small)
    rows = compact(lengths, got.reshape(NCP, SEG, F), got_small)
    full, risk = main(*rows, factors, aversion)
    load, thr, dates = give_back(place(lengths, full))
    return (load.T, thr.reshape(ROWS), dates.T, risk[:, 0])


def solution(mesh):
    in_specs = (P("sc", None), P("cp", None), P("cp"), P("cp", None), P(), P())
    out_specs = (P("cp", "sc"), P("cp"), P("cp", None), P())
    return jax.shard_map(
        per_device, mesh=mesh, in_specs=in_specs, out_specs=out_specs, check_vma=False
    )
```

```python
import math

import jax
import jax.numpy as jnp
from jax import lax
from jax.experimental import pallas as pl
from jax.experimental.pallas import tpu as pltpu
from jax.sharding import PartitionSpec as P

MESH = pl.DeviceIdType.MESH
NCP = 16
NSC = 8
F = 256
ROWS = 4096
S = 4096
CAP = 2176
SEG = ROWS // NCP
LIVE = 32768
SCEN = 32768
ST = 512
CHUNKS = ((0, 768), (768, 768), (1536, 640))
ROOT_HALF = 0.7071067811865476
LOG2E = 1.4426950408889634
FAR = -3.1
TAIL = (-0.750217616, 0.756257034, -1.37553279, 0.0025935648)
BF = jnp.bfloat16
F32 = jnp.float32


def spots(lengths_ref, position):
    start = jnp.int32(0)
    out = []
    for block in range(NCP):
        live = lengths_ref[block]
        tiles = (live + 15) >> 4
        offset = (position - block + NCP) % NCP
        out.append((start, offset, live))
        start = start + ((tiles - offset + 15) >> 4)
    return out


def exchange_kernel(tiles, small, got, got_small, sends, recvs, sends_s, recvs_s, sends_b, recvs_b, own):
    me = lax.axis_index("cp")
    sc = lax.axis_index("sc")
    core = sc % 2
    sibling = sc + 1 - 2 * core
    barrier = pltpu.get_barrier_semaphore()

    def greet(k, _):
        pl.semaphore_signal(barrier, inc=1, device_id=((me + k) % NCP, sc), device_id_type=MESH)
        return 0

    lax.fori_loop(1, NCP, greet, 0)
    pl.semaphore_signal(barrier, inc=1, device_id=(me, sibling), device_id_type=MESH)
    pl.semaphore_wait(barrier, NCP)

    half = pl.ds(core * 8, 8)

    def row_copy(k):
        peer = (me + k) % NCP
        return pltpu.make_async_remote_copy(
            src_ref=tiles.at[half, (peer - me + NCP) % NCP],
            dst_ref=got.at[me, half],
            send_sem=sends.at[k],
            recv_sem=recvs.at[k],
            device_id=(peer, sc),
            device_id_type=MESH,
        )

    def small_copy(k):
        peer = (me + k) % NCP
        return pltpu.make_async_remote_copy(
            src_ref=small.at[(peer - me + NCP) % NCP],
            dst_ref=got_small.at[me],
            send_sem=sends_s.at[k],
            recv_sem=recvs_s.at[k],
            device_id=(peer, sc),
            device_id_type=MESH,
        )

    def forward(k):
        source = (me - k + NCP) % NCP
        return pltpu.make_async_remote_copy(
            src_ref=got.at[source, half],
            dst_ref=got.at[source, half],
            send_sem=sends_b.at[k],
            recv_sem=recvs_b.at[k],
            device_id=(me, sibling),
            device_id_type=MESH,
        )

    def start(k, _):
        row_copy(k).start()
        small_copy(k).start()
        return 0

    lax.fori_loop(1, NCP, start, 0)
    mine = pltpu.make_async_copy(tiles.at[:, 0], got.at[me], own.at[0])
    mine.start()
    mine_small = pltpu.make_async_copy(small.at[0], got_small.at[me], own.at[1])
    mine_small.start()

    def pass_on(k, _):
        row_copy(k).wait_recv()
        forward(k).start()
        return 0

    lax.fori_loop(1, NCP, pass_on, 0)
    mine.wait()
    mine_small.wait()

    def finish(k, _):
        row_copy(k).wait_send()
        small_copy(k).wait()
        forward(k).wait()
        return 0

    lax.fori_loop(1, NCP, finish, 0)


def exchange(tiles, small):
    any_spec = pl.BlockSpec(memory_space=pl.ANY)
    return pl.pallas_call(
        exchange_kernel,
        out_shape=(
            jax.ShapeDtypeStruct((NCP, 16, 16, F), BF),
            jax.ShapeDtypeStruct((NCP, 16, SEG), BF),
        ),
        in_specs=[any_spec] * 2,
        out_specs=[any_spec] * 2,
        scratch_shapes=[pltpu.SemaphoreType.DMA((NCP,))] * 6 + [pltpu.SemaphoreType.DMA((2,))],
        compiler_params=pltpu.CompilerParams(collective_id=0, has_side_effects=True),
        name="exchange",
    )(tiles, small)


def double_cdf(u):
    far = TAIL[3]
    for coef in TAIL[2::-1]:
        far = far * u + coef
    return jnp.where(u < FAR, jnp.exp2(far), 1.0 + lax.erf(u))


def run(first, last, act):
    def body(k, _):
        act(k)
        return 0

    lax.fori_loop(first, last, body, 0)


def compact_kernel(lengths, got, got_small, comp, shift, slope, expo, expo_t, wide):
    comp[...] = jnp.zeros_like(comp)
    wide[...] = jnp.zeros_like(wide)
    index = lax.broadcasted_iota(jnp.int32, (SEG, 128), 0)
    lane = lax.broadcasted_iota(jnp.int32, (SEG, 128), 1)
    for block, (start, offset, live) in enumerate(spots(lengths, lax.axis_index("cp"))):
        at = pl.ds(pl.multiple_of(start * 16, 16), SEG)
        comp[at, :] = got[block]
        part = got_small[block].astype(F32)
        part = jnp.concatenate([part, jnp.zeros((112, SEG), F32)], axis=0).T
        row = (offset + 16 * (index // 16)) * 16 + index % 16
        keep = (row < live) | (lane >= 8)
        wide[at, :] = jnp.where(keep, part, 0.0)

    def scale(i, _):
        at = pl.ds(pl.multiple_of(i * 128, 128), 128)
        rows = comp[at, :].astype(F32)
        total = jnp.sum(rows * rows, axis=1, keepdims=True)
        by = lax.rsqrt(1.0 + total) * ROOT_HALF
        slope[at, :] = jnp.broadcast_to(by, (128, 128))
        part = wide[at, :]
        shift[at, :] = jnp.broadcast_to(part[:, 8:9] * by, (128, 128))
        expo[at, :] = part.astype(BF)
        expo_t[:, at] = part.T[0:16, :].astype(BF)
        return 0

    lax.fori_loop(0, CAP // 128, scale, 0)


def compact(lengths, got, got_small):
    vmem = pl.BlockSpec(memory_space=pltpu.VMEM)
    return pl.pallas_call(
        compact_kernel,
        out_shape=(
            jax.ShapeDtypeStruct((CAP + SEG, F), BF),
            jax.ShapeDtypeStruct((CAP, 128), F32),
            jax.ShapeDtypeStruct((CAP, 128), F32),
            jax.ShapeDtypeStruct((CAP, 128), BF),
            jax.ShapeDtypeStruct((16, CAP), BF),
        ),
        in_specs=[pl.BlockSpec(memory_space=pltpu.SMEM), vmem, vmem],
        out_specs=[vmem] * 5,
        scratch_shapes=[pltpu.VMEM((CAP + SEG, 128), F32)],
        name="compact",
    )(lengths, got, got_small)


def main_kernel(
    comp, shift, slope, expo, expo_t, factors, aversion, lengths, load_out, thr_out, expo_out, risk,
    full, pack, back, prob, loss, parts, mine, every, stats, weights, turned,
    expo_acc, dates, dates_in, date_sum, date_all,
    load_acc, lat_acc, thr_acc, grads, pair, sum_l, near_l, thr_line, thr_pair, thr_sum, thr_near,
    sends, recvs, sends_g, recvs_g, sends_z, recvs_z, sends_d, recvs_d, sends_e, recvs_e,
    sends_a, recvs_a, sends_b, recvs_b, sends_t, recvs_t, sends_c, recvs_c,
):
    me = lax.axis_index("cp")
    sc = lax.axis_index("sc")
    core = sc % 2
    z = sc // 2
    sibling = sc + 1 - 2 * core
    width = S // NCP
    barrier = pltpu.get_barrier_semaphore()
    run(1, NCP, lambda k: pl.semaphore_signal(barrier, inc=1, device_id=((me + k) % NCP, sc), device_id_type=MESH))
    run(1, NSC, lambda k: pl.semaphore_signal(barrier, inc=1, device_id=(me, (sc + k) % NSC), device_id_type=MESH))

    def remote(src, dst, send, recv, to):
        return pltpu.make_async_remote_copy(
            src_ref=src, dst_ref=dst, send_sem=send, recv_sem=recv, device_id=to, device_id_type=MESH
        )

    def latent(first, count, cols):
        rows = pl.ds(first, count)
        project = lax.dot_general(
            comp[rows, :], factors[cols, :], (((1,), (1,)), ((), ())), preferred_element_type=F32
        )
        a = jnp.concatenate([shift[rows, :]] * (ST // 128), axis=1)
        b = jnp.concatenate([slope[rows, :]] * (ST // 128), axis=1)
        return a - project * b

    def ahead(step):
        cols = pl.ds(pl.multiple_of(step * ST, ST), ST)
        for first, count in CHUNKS:
            prob[pl.ds(first, count), cols] = double_cdf(latent(first, count, cols)).astype(BF)
        loss[:, cols] = jnp.dot(expo_t[...], prob[:, cols], preferred_element_type=F32)[0:8, :]

    run(0, S // ST, ahead)
    pl.semaphore_wait(barrier, NCP + NSC - 2)

    def part_of(position):
        return pl.ds(pl.multiple_of(position * width, width), width)

    def scatter(k):
        peer = (me + k) % NCP
        return remote(loss.at[:, part_of(peer)], parts.at[me], sends.at[k], recvs.at[k], (peer, sc))

    def gather(k):
        return remote(mine, every.at[:, part_of(me)], sends_g.at[k], recvs_g.at[k], ((me + k) % NCP, sc))

    def share(k):
        return remote(stats.at[sc], stats.at[sc], sends_z.at[k], recvs_z.at[k], (me, (sc + k) % NSC))

    run(1, NCP, lambda k: scatter(k).start())
    parts[me] = loss[:, part_of(me)]
    at_date = lax.broadcasted_iota(jnp.int32, (8, 128), 0)
    averse = jnp.zeros((8, 128), F32)
    for t in range(8):
        averse = jnp.where(at_date == t, aversion[t], averse)
    run(1, NCP, lambda k: scatter(k).wait_recv())
    total = parts[0]
    for i in range(1, NCP):
        total = total + parts[i]
    score = jnp.concatenate([averse] * (width // 128), axis=1) * (total * (0.5 / LIVE))
    mine[...] = score
    run(1, NCP, lambda k: gather(k).start())
    every[:, part_of(me)] = score
    run(1, NCP, lambda k: gather(k).wait_recv())
    scores = every[...]
    top = jnp.max(scores, axis=1, keepdims=True)
    raised = jnp.exp(scores - top)
    mass = jnp.sum(raised, axis=1, keepdims=True)
    stats[sc, 0:8, :] = jnp.broadcast_to(top, (8, 128))
    stats[sc, 8:16, :] = jnp.broadcast_to(mass, (8, 128))
    run(1, NSC, lambda k: share(k).start())
    weights[...] = jnp.concatenate([raised, jnp.zeros((8, S), F32)], axis=0).astype(BF)

    expo_acc[...] = jnp.zeros_like(expo_acc)

    def expose(step):
        cols = pl.ds(pl.multiple_of(step * ST, ST), ST)
        turned[:, 0:16] = weights[:, cols].astype(F32).T.astype(BF)
        expo_acc[...] += jnp.dot(prob[:, cols], turned[:, 0:16], preferred_element_type=F32)

    run(0, S // ST, expose)
    run(1, NSC, lambda k: share(k).wait_recv())
    best = stats[0, 0:8, :]
    for i in range(1, NSC):
        best = jnp.maximum(best, stats[i, 0:8, :])
    heap = jnp.zeros((8, 128), F32)
    for i in range(NSC):
        heap = heap + stats[i, 8:16, :] * jnp.exp(stats[i, 0:8, :] - best)
    final = jnp.exp(every[...] - best[:, 0:1]) / heap[:, 0:1]
    weights[...] = jnp.concatenate([final, jnp.zeros((8, S), F32)], axis=0).astype(BF)
    risk[...] = (best + jnp.log(heap / SCEN)) / averse
    run(1, NCP, lambda k: scatter(k).wait_send())
    run(1, NCP, lambda k: gather(k).wait_send())
    run(1, NSC, lambda k: share(k).wait_send())
    own_scale = jnp.exp(stats[sc, 0:8, :] - best) / heap * (0.5 / LIVE)
    for i in range(CAP // 128):
        block = jnp.concatenate(
            [expo_acc[128 * i : 128 * (i + 1), :], jnp.zeros((128, 112), F32)], axis=1
        ).T
        for j in range(NSC):
            dates[j, :, 128 * i : 128 * (i + 1)] = block[j : j + 1, :] * own_scale[j : j + 1, :]

    def date_out(k):
        peer = (sc + k) % NSC
        return remote(dates.at[peer], dates_in.at[k], sends_d.at[k], recvs_d.at[k], (me, peer))

    def date_share(k):
        return remote(date_sum, date_all.at[sc], sends_e.at[k], recvs_e.at[k], (me, (sc + k) % NSC))

    run(1, NSC, lambda k: date_out(k).start())

    def pair_copy(c, k):
        first, count = CHUNKS[c]
        at = pl.ds(first, count)
        return remote(
            grads.at[((z + k) % 4) * 2 + 1 - core, :, at], pair.at[k, :, at],
            sends_a.at[c, k], recvs_a.at[c, k], (me, sibling),
        )

    def thr_pair_copy(c):
        at = pl.ds(*CHUNKS[c])
        return remote(thr_line.at[:, at], thr_pair.at[:, at], sends_a.at[c, 4], recvs_a.at[c, 4], (me, sibling))

    def near_copy(c, k):
        at = pl.ds(*CHUNKS[c])
        return remote(
            sum_l.at[k, :, at], near_l.at[k, :, at],
            sends_b.at[c, k], recvs_b.at[c, k], (me, ((z + k) % 4) * 2 + core),
        )

    def thr_near_copy(c, k):
        at = pl.ds(*CHUNKS[c])
        return remote(
            thr_sum.at[:, at], thr_near.at[k, :, at],
            sends_t.at[c, k], recvs_t.at[c, k], (me, ((z + k) % 4) * 2 + core),
        )

    def back_steps(c, low, high):
        first, count = CHUNKS[c]
        rows = pl.ds(first, count)
        acc = pl.ds(0, count)

        def step(i):
            cols = pl.ds(pl.multiple_of(i * ST, ST), ST)
            pull = jnp.dot(expo[rows, 0:16], weights[:, cols], preferred_element_type=F32)
            u = latent(first, count, cols)
            heavy = pull * jnp.exp2(u * u * (-LOG2E))
            lat = heavy * u
            lat_sum = lat[:, 0:128]
            thr_part = heavy[:, 0:128]
            for k in range(1, ST // 128):
                lat_sum = lat_sum + lat[:, k * 128 : (k + 1) * 128]
                thr_part = thr_part + heavy[:, k * 128 : (k + 1) * 128]
            lat_acc[acc, :] += lat_sum
            thr_acc[acc, :] += thr_part
            load_acc[acc, :] += jnp.dot(heavy.astype(BF), factors[cols, :], preferred_element_type=F32)

        run(low, high, step)

    def fold(c):
        first, count = CHUNKS[c]
        scale = 1.0 / (LIVE * math.sqrt(2.0 * math.pi))

        def one(i):
            rows = pl.ds(pl.multiple_of(first + i * 128, 128), 128)
            acc = pl.ds(pl.multiple_of(i * 128, 128), 128)
            by = slope[rows, 0:1] * math.sqrt(2.0)
            lat = jnp.sum(lat_acc[acc, :], axis=1, keepdims=True) * (scale * math.sqrt(2.0))
            thr = jnp.sum(thr_acc[acc, :], axis=1, keepdims=True) * scale * by
            grad = -(load_acc[acc, :] * (scale * by)) - (lat * by * by) * comp[rows, :].astype(F32)
            flat = grad.T
            for j in range(NSC):
                grads[j, :, rows] = flat[32 * j : 32 * (j + 1), :]
            thr_line[:, rows] = jnp.broadcast_to(thr, (128, 128)).T[0:1, :]

        run(0, count // 128, one)
        for k in (2, 1, 3, 0):
            pair_copy(c, k).start()
        thr_pair_copy(c).start()

    def pair_up(c):
        first, count = CHUNKS[c]
        at = pl.ds(first, count)
        for k in (2, 1, 3):
            pair_copy(c, k).wait_recv()
            sum_l[k, :, at] = (grads[((z + k) % 4) * 2 + core, :, at] + pair[k, :, at]).astype(BF)
            near_copy(c, k).start()
        thr_pair_copy(c).wait_recv()
        thr_sum[:, at] = thr_line[:, at] + thr_pair[:, at]
        for k in (2, 1, 3):
            thr_near_copy(c, k).start()
        pair_copy(c, 0).wait_recv()

    def near_up(c):
        first, count = CHUNKS[c]
        at = pl.ds(first, count)
        held = grads[sc, :, at] + pair[0, :, at]
        thr = thr_sum[:, at]
        for k in (1, 3, 2):
            near_copy(c, k).wait_recv()
            thr_near_copy(c, k).wait_recv()
            held = held + near_l[k, :, at].astype(F32)
            thr = thr + thr_near[k, :, at]
        for i in range(count // 128):
            part = slice(128 * i, 128 * (i + 1))
            full[first // 128 + i, 0:32, :] = held[:, part]
            full[first // 128 + i, 40:41, :] = thr[:, part]

    full[CAP // 128 :, :, :] = jnp.zeros((3, 48, 128), F32)
    full[0 : CAP // 128, 40:48, :] = jnp.zeros((CAP // 128, 8, 128), F32)
    steps = S // ST
    for c in range(len(CHUNKS)):
        load_acc[...] = jnp.zeros_like(load_acc)
        lat_acc[...] = jnp.zeros_like(lat_acc)
        thr_acc[...] = jnp.zeros_like(thr_acc)
        back_steps(c, 0, steps // 2)
        if c == 0:
            run(1, NSC, lambda k: date_out(k).wait_recv())
            line = dates[sc]
            for k in range(1, NSC):
                line = line + dates_in[k]
            date_sum[...] = line
            run(1, NSC, lambda k: date_share(k).start())
            date_all[sc] = line
        else:
            pair_up(c - 1)
        back_steps(c, steps // 2, steps)
        if c:
            near_up(c - 1)
        fold(c)
    last = len(CHUNKS) - 1
    run(1, NSC, lambda k: date_share(k).wait_recv())
    for j in range(NSC):
        for i in range(CAP // 128):
            full[i, 32 + j : 33 + j, :] = date_all[j, :, 128 * i : 128 * (i + 1)]
    pair_up(last)
    run(1, NSC, lambda k: (date_out(k).wait_send(), date_share(k).wait_send()))
    near_up(last)
    lane = lax.broadcasted_iota(jnp.int32, (48, SEG), 1)
    for block, (start, offset, live) in enumerate(spots(lengths, me)):
        tile = start >> 3
        piece = jnp.concatenate([full[tile], full[tile + 1], full[tile + 2]], axis=1)
        part = jnp.full((48, 384), start & 7, jnp.int32)
        for bit in (1, 2, 4):
            piece = jnp.where(part & bit != 0, pltpu.roll(piece, 384 - 16 * bit, 1), piece)
        row = (offset + 16 * (lane // 16)) * 16 + lane % 16
        pack[block] = jnp.where(row < live, piece[:, 0:SEG], 0.0).astype(BF)

    def back_copy(k):
        peer = (me + k) % NCP
        return remote(pack.at[peer], back.at[(me - peer + NCP) % NCP], sends_c.at[k], recvs_c.at[k], (peer, sc))

    run(1, NCP, lambda k: back_copy(k).start())
    back[0] = pack[me]
    for c in range(len(CHUNKS)):
        for k in range(4):
            pair_copy(c, k).wait_send()
        thr_pair_copy(c).wait_send()
        for k in range(1, 4):
            near_copy(c, k).wait_send()
            thr_near_copy(c, k).wait_send()
    run(1, NCP, lambda k: back_copy(k).wait_recv())
    group = lax.broadcasted_iota(jnp.int32, (48, 128), 1) // 16
    for g in range(2):
        for h in range(2):
            held = [back[8 * g + q, :, 128 * h : 128 * (h + 1)].astype(F32) for q in range(8)]
            for s in range(8):
                mixed = held[s]
                for q in range(8):
                    if q != s:
                        moved = pltpu.roll(held[q], (16 * (q - s)) % 128, 1)
                        mixed = jnp.where(group == q, moved, mixed)
                tile = 2 * (8 * h + s) + g
                at = slice(128 * tile, 128 * (tile + 1))
                load_out[:, at] = mixed[0:32, :]
                expo_out[:, at] = mixed[32:40, :]
                thr_out[:, at] = mixed[40:41, :]
    run(1, NCP, lambda k: back_copy(k).wait_send())


def main(comp, shift, slope, expo, expo_t, factors, aversion, lengths):
    vmem = pl.BlockSpec(memory_space=pltpu.VMEM)
    dma = pltpu.SemaphoreType.DMA
    parts = len(CHUNKS)
    most = max(count for _, count in CHUNKS)
    return pl.pallas_call(
        main_kernel,
        out_shape=(
            jax.ShapeDtypeStruct((32, ROWS), F32),
            jax.ShapeDtypeStruct((1, ROWS), F32),
            jax.ShapeDtypeStruct((NSC, ROWS), F32),
            jax.ShapeDtypeStruct((8, 128), F32),
        ),
        in_specs=[vmem] * 6 + [pl.BlockSpec(memory_space=pltpu.SMEM)] * 2,
        out_specs=[vmem] * 4,
        scratch_shapes=[
            pltpu.VMEM((CAP // 128 + 3, 48, 128), F32),
            pltpu.VMEM((NCP, 48, SEG), BF),
            pltpu.VMEM((NCP, 48, SEG), BF),
            pltpu.VMEM((CAP, S), BF),
            pltpu.VMEM((8, S), F32),
            pltpu.VMEM((NCP, 8, S // NCP), F32),
            pltpu.VMEM((8, S // NCP), F32),
            pltpu.VMEM((8, S), F32),
            pltpu.VMEM((NSC, 16, 128), F32),
            pltpu.VMEM((16, S), BF),
            pltpu.VMEM((ST, 128), BF),
            pltpu.VMEM((CAP, 16), F32),
            pltpu.VMEM((NSC, 1, CAP), F32),
            pltpu.VMEM((NSC, 1, CAP), F32),
            pltpu.VMEM((1, CAP), F32),
            pltpu.VMEM((NSC, 1, CAP), F32),
            pltpu.VMEM((most, F), F32),
            pltpu.VMEM((most, 128), F32),
            pltpu.VMEM((most, 128), F32),
            pltpu.VMEM((NSC, 32, CAP), F32),
            pltpu.VMEM((4, 32, CAP), F32),
            pltpu.VMEM((4, 32, CAP), BF),
            pltpu.VMEM((4, 32, CAP), BF),
            pltpu.VMEM((1, CAP), F32),
            pltpu.VMEM((1, CAP), F32),
            pltpu.VMEM((1, CAP), F32),
            pltpu.VMEM((4, 1, CAP), F32),
            dma((NCP,)),
            dma((NCP,)),
            dma((NCP,)),
            dma((NCP,)),
            dma((NSC,)),
            dma((NSC,)),
            dma((NSC,)),
            dma((NSC,)),
            dma((NSC,)),
            dma((NSC,)),
            dma((parts, 5)),
            dma((parts, 5)),
            dma((parts, 4)),
            dma((parts, 4)),
            dma((parts, 4)),
            dma((parts, 4)),
            dma((NCP,)),
            dma((NCP,)),
        ],
        compiler_params=pltpu.CompilerParams(
            collective_id=1, has_side_effects=True, vmem_limit_bytes=58 * 2**20
        ),
        name="main",
    )(comp, shift, slope, expo, expo_t, factors, aversion, lengths)


def per_device(factors, loadings, thresholds, exposures, aversion, lengths):
    tiles = loadings.reshape(16, NCP, 16, F)
    small = jnp.concatenate(
        [exposures.T, thresholds[None, :], jnp.zeros((7, ROWS), BF)], axis=0
    )
    small = small.reshape(16, 16, NCP, 16).transpose(2, 0, 1, 3).reshape(NCP, 16, SEG)
    got, got_small = exchange(tiles, small)
    rows = compact(lengths, got.reshape(NCP, SEG, F), got_small)
    load, thr, dates, risk = main(*rows, factors, aversion, lengths)
    return (load.T, thr.reshape(ROWS), dates.T, risk[:, 0])


def solution(mesh):
    in_specs = (P("sc", None), P("cp", None), P("cp"), P("cp", None), P(), P())
    out_specs = (P("cp", "sc"), P("cp"), P("cp", None), P())
    return jax.shard_map(
        per_device, mesh=mesh, in_specs=in_specs, out_specs=out_specs, check_vma=False
    )
```

```python
import math

import jax
import jax.numpy as jnp
from jax import lax
from jax.experimental import pallas as pl
from jax.experimental.pallas import tpu as pltpu
from jax.sharding import PartitionSpec as P

MESH = pl.DeviceIdType.MESH
NCP = 16
NSC = 8
F = 256
ROWS = 4096
S = 4096
CAP = 2176
SEG = ROWS // NCP
LIVE = 32768
SCEN = 32768
ST = 512
CHUNKS = ((0, 768), (768, 768), (1536, 640))
ROOT_HALF = 0.7071067811865476
LOG2E = 1.4426950408889634
FAR = -3.1
TAIL = (-0.750217616, 0.756257034, -1.37553279, 0.0025935648)
BF = jnp.bfloat16
F32 = jnp.float32


def spots(lengths_ref, position):
    start = jnp.int32(0)
    out = []
    for block in range(NCP):
        live = lengths_ref[block]
        tiles = (live + 15) >> 4
        offset = (position - block + NCP) % NCP
        out.append((start, offset, live))
        start = start + ((tiles - offset + 15) >> 4)
    return out


def double_cdf(u):
    far = TAIL[3]
    for coef in TAIL[2::-1]:
        far = far * u + coef
    return jnp.where(u < FAR, jnp.exp2(far), 1.0 + lax.erf(u))


def run(first, last, act):
    def body(k, _):
        act(k)
        return 0

    lax.fori_loop(first, last, body, 0)


def main_kernel(
    tiles, expo_in, thr_in, factors, aversion, lengths, load_out, thr_out, expo_out, risk,
    got, small, got_small, wide, comp, shift, slope, expo, expo_t, table, lives, full, pack, back, prob, loss, parts, mine, every, stats, weights, turned,
    expo_acc, dates, dates_in, date_sum, date_all,
    load_acc, lat_acc, thr_acc, grads, pair, sum_l, near_l, thr_line, thr_pair, thr_sum, thr_near,
    sends, recvs, sends_g, recvs_g, sends_z, recvs_z, sends_d, recvs_d, sends_e, recvs_e,
    sends_a, recvs_a, sends_b, recvs_b, sends_t, recvs_t, sends_c, recvs_c,
    sends_x, recvs_x, sends_s, recvs_s, sends_y, recvs_y, own,
):
    me = lax.axis_index("cp")
    sc = lax.axis_index("sc")
    core = sc % 2
    z = sc // 2
    sibling = sc + 1 - 2 * core
    width = S // NCP
    barrier = pltpu.get_barrier_semaphore()
    run(1, NCP, lambda k: pl.semaphore_signal(barrier, inc=1, device_id=((me + k) % NCP, sc), device_id_type=MESH))
    run(1, NSC, lambda k: pl.semaphore_signal(barrier, inc=1, device_id=(me, (sc + k) % NSC), device_id_type=MESH))

    def remote(src, dst, send, recv, to):
        return pltpu.make_async_remote_copy(
            src_ref=src, dst_ref=dst, send_sem=send, recv_sem=recv, device_id=to, device_id_type=MESH
        )

    half = core * 8

    def row_copy(k):
        peer = (me + k) % NCP
        return remote(
            tiles.at[pl.ds(half, 8), (peer - me + NCP) % NCP], got.at[pl.ds(me * 16 + half, 8)],
            sends_x.at[k], recvs_x.at[k], (peer, sc),
        )

    def small_copy(k):
        peer = (me + k) % NCP
        return remote(
            small.at[(peer - me + NCP) % NCP], got_small.at[me], sends_s.at[k], recvs_s.at[k], (peer, sc)
        )

    def pass_on(k):
        at = pl.ds(((me - k + NCP) % NCP) * 16 + half, 8)
        return remote(got.at[at], got.at[at], sends_y.at[k], recvs_y.at[k], (me, sibling))

    chunk_of = lax.broadcasted_iota(jnp.int32, (16, 128), 1) // 16
    limits = jnp.broadcast_to(thr_in[...].astype(F32), (8, ROWS))
    raw = jnp.concatenate([expo_in[...].astype(F32), limits], axis=0)
    for t in range(NCP):
        for h in range(2):
            mixed = None
            for q in range(8):
                tile = 2 * (8 * h + q) + t // 8
                moved = pltpu.roll(raw[:, 128 * tile : 128 * (tile + 1)], (16 * (q - t % 8)) % 128, 1)
                mixed = moved if mixed is None else jnp.where(chunk_of == q, moved, mixed)
            small[t, :, 128 * h : 128 * (h + 1)] = mixed.astype(BF)

    pl.semaphore_wait(barrier, NCP + NSC - 2)
    run(1, NCP, lambda k: (row_copy(k).start(), small_copy(k).start()))
    mine_rows = pltpu.make_async_copy(tiles.at[:, 0], got.at[pl.ds(me * 16, 16)], own.at[0])
    mine_rows.start()
    got_small[me] = small[0]

    places = spots(lengths, me)

    def tabulate(k):
        block = jnp.int32(0)
        begin = jnp.int32(0)
        offset = places[0][1]
        live = places[0][2]
        for i in range(1, NCP):
            later = k >= places[i][0]
            block = jnp.where(later, i, block)
            begin = jnp.where(later, places[i][0], begin)
            offset = jnp.where(later, places[i][1], offset)
            live = jnp.where(later, places[i][2], live)
        slot = jnp.minimum(k - begin, 15)
        table[k] = block * 16 + slot
        lives[k] = live - (offset + 16 * slot) * 16 - 32768 * jnp.where(k - begin > 15, 1, 0)

    run(0, CAP // 16, tabulate)
    run(1, NCP, lambda k: small_copy(k).wait_recv())
    for block in range(NCP):
        part = got_small[block].astype(F32)
        part = jnp.concatenate([part, jnp.zeros((112, SEG), F32)], axis=0).T
        for slot in range(16):
            wide[block * 16 + slot] = part[16 * slot : 16 * (slot + 1), :]
    run(1, NCP, lambda k: (row_copy(k).wait_recv(), pass_on(k).start()))
    mine_rows.wait()
    run(1, NCP, lambda k: (row_copy(k).wait_send(), small_copy(k).wait_send(), pass_on(k).wait()))

    row_of = lax.broadcasted_iota(jnp.int32, (16, 128), 0)
    lane_of = lax.broadcasted_iota(jnp.int32, (16, 128), 1)

    def compact(i):
        at = pl.ds(pl.multiple_of(i * 128, 128), 128)
        rows = jnp.concatenate([got[table[8 * i + q]] for q in range(8)], axis=0)
        part = jnp.concatenate(
            [
                jnp.where((row_of < lives[8 * i + q]) | (lane_of >= 8), wide[table[8 * i + q]], 0.0)
                for q in range(8)
            ],
            axis=0,
        )
        comp[at, :] = rows
        rows = rows.astype(F32)
        total = jnp.sum(rows * rows, axis=1, keepdims=True)
        by = lax.rsqrt(1.0 + total) * ROOT_HALF
        slope[at, :] = jnp.broadcast_to(by, (128, 128))
        shift[at, :] = jnp.broadcast_to(part[:, 8:9] * by, (128, 128))
        expo[at, :] = part.astype(BF)
        expo_t[:, at] = part.T[0:16, :].astype(BF)

    run(0, CAP // 128, compact)

    def latent(first, count, cols):
        rows = pl.ds(first, count)
        project = lax.dot_general(
            comp[rows, :], factors[cols, :], (((1,), (1,)), ((), ())), preferred_element_type=F32
        )
        a = jnp.concatenate([shift[rows, :]] * (ST // 128), axis=1)
        b = jnp.concatenate([slope[rows, :]] * (ST // 128), axis=1)
        return a - project * b

    def ahead(step):
        cols = pl.ds(pl.multiple_of(step * ST, ST), ST)
        for first, count in CHUNKS:
            prob[pl.ds(first, count), cols] = double_cdf(latent(first, count, cols)).astype(BF)
        loss[:, cols] = jnp.dot(expo_t[...], prob[:, cols], preferred_element_type=F32)[0:8, :]

    run(0, S // ST, ahead)

    def part_of(position):
        return pl.ds(pl.multiple_of(position * width, width), width)

    def scatter(k):
        peer = (me + k) % NCP
        return remote(loss.at[:, part_of(peer)], parts.at[me], sends.at[k], recvs.at[k], (peer, sc))

    def gather(k):
        return remote(mine, every.at[:, part_of(me)], sends_g.at[k], recvs_g.at[k], ((me + k) % NCP, sc))

    def share(k):
        return remote(stats.at[sc], stats.at[sc], sends_z.at[k], recvs_z.at[k], (me, (sc + k) % NSC))

    run(1, NCP, lambda k: scatter(k).start())
    parts[me] = loss[:, part_of(me)]
    at_date = lax.broadcasted_iota(jnp.int32, (8, 128), 0)
    averse = jnp.zeros((8, 128), F32)
    for t in range(8):
        averse = jnp.where(at_date == t, aversion[t], averse)
    run(1, NCP, lambda k: scatter(k).wait_recv())
    total = parts[0]
    for i in range(1, NCP):
        total = total + parts[i]
    score = jnp.concatenate([averse] * (width // 128), axis=1) * (total * (0.5 / LIVE))
    mine[...] = score
    run(1, NCP, lambda k: gather(k).start())
    every[:, part_of(me)] = score
    run(1, NCP, lambda k: gather(k).wait_recv())
    scores = every[...]
    top = jnp.max(scores, axis=1, keepdims=True)
    raised = jnp.exp(scores - top)
    mass = jnp.sum(raised, axis=1, keepdims=True)
    stats[sc, 0:8, :] = jnp.broadcast_to(top, (8, 128))
    stats[sc, 8:16, :] = jnp.broadcast_to(mass, (8, 128))
    run(1, NSC, lambda k: share(k).start())
    weights[...] = jnp.concatenate([raised, jnp.zeros((8, S), F32)], axis=0).astype(BF)

    expo_acc[...] = jnp.zeros_like(expo_acc)

    def expose(step):
        cols = pl.ds(pl.multiple_of(step * ST, ST), ST)
        turned[:, 0:16] = weights[:, cols].astype(F32).T.astype(BF)
        expo_acc[...] += jnp.dot(prob[:, cols], turned[:, 0:16], preferred_element_type=F32)

    run(0, S // ST, expose)
    run(1, NSC, lambda k: share(k).wait_recv())
    best = stats[0, 0:8, :]
    for i in range(1, NSC):
        best = jnp.maximum(best, stats[i, 0:8, :])
    heap = jnp.zeros((8, 128), F32)
    for i in range(NSC):
        heap = heap + stats[i, 8:16, :] * jnp.exp(stats[i, 0:8, :] - best)
    final = jnp.exp(every[...] - best[:, 0:1]) / heap[:, 0:1]
    weights[...] = jnp.concatenate([final, jnp.zeros((8, S), F32)], axis=0).astype(BF)
    risk[...] = (best + jnp.log(heap / SCEN)) / averse
    run(1, NCP, lambda k: scatter(k).wait_send())
    run(1, NCP, lambda k: gather(k).wait_send())
    run(1, NSC, lambda k: share(k).wait_send())
    own_scale = jnp.exp(stats[sc, 0:8, :] - best) / heap * (0.5 / LIVE)
    for i in range(CAP // 128):
        block = jnp.concatenate(
            [expo_acc[128 * i : 128 * (i + 1), :], jnp.zeros((128, 112), F32)], axis=1
        ).T
        for j in range(NSC):
            dates[j, :, 128 * i : 128 * (i + 1)] = block[j : j + 1, :] * own_scale[j : j + 1, :]

    def date_out(k):
        peer = (sc + k) % NSC
        return remote(dates.at[peer], dates_in.at[k], sends_d.at[k], recvs_d.at[k], (me, peer))

    def date_share(k):
        return remote(date_sum, date_all.at[sc], sends_e.at[k], recvs_e.at[k], (me, (sc + k) % NSC))

    run(1, NSC, lambda k: date_out(k).start())

    def pair_copy(c, k):
        first, count = CHUNKS[c]
        at = pl.ds(first, count)
        return remote(
            grads.at[((z + k) % 4) * 2 + 1 - core, :, at], pair.at[k, :, at],
            sends_a.at[c, k], recvs_a.at[c, k], (me, sibling),
        )

    def thr_pair_copy(c):
        at = pl.ds(*CHUNKS[c])
        return remote(thr_line.at[:, at], thr_pair.at[:, at], sends_a.at[c, 4], recvs_a.at[c, 4], (me, sibling))

    def near_copy(c, k):
        at = pl.ds(*CHUNKS[c])
        return remote(
            sum_l.at[k, :, at], near_l.at[k, :, at],
            sends_b.at[c, k], recvs_b.at[c, k], (me, ((z + k) % 4) * 2 + core),
        )

    def thr_near_copy(c, k):
        at = pl.ds(*CHUNKS[c])
        return remote(
            thr_sum.at[:, at], thr_near.at[k, :, at],
            sends_t.at[c, k], recvs_t.at[c, k], (me, ((z + k) % 4) * 2 + core),
        )

    def back_steps(c, low, high):
        first, count = CHUNKS[c]
        rows = pl.ds(first, count)
        acc = pl.ds(0, count)

        def step(i):
            cols = pl.ds(pl.multiple_of(i * ST, ST), ST)
            pull = jnp.dot(expo[rows, 0:16], weights[:, cols], preferred_element_type=F32)
            u = latent(first, count, cols)
            heavy = pull * jnp.exp2(u * u * (-LOG2E))
            lat = heavy * u
            lat_sum = lat[:, 0:128]
            thr_part = heavy[:, 0:128]
            for k in range(1, ST // 128):
                lat_sum = lat_sum + lat[:, k * 128 : (k + 1) * 128]
                thr_part = thr_part + heavy[:, k * 128 : (k + 1) * 128]
            lat_acc[acc, :] += lat_sum
            thr_acc[acc, :] += thr_part
            load_acc[acc, :] += jnp.dot(heavy.astype(BF), factors[cols, :], preferred_element_type=F32)

        run(low, high, step)

    def fold(c):
        first, count = CHUNKS[c]
        scale = 1.0 / (LIVE * math.sqrt(2.0 * math.pi))

        def one(i):
            rows = pl.ds(pl.multiple_of(first + i * 128, 128), 128)
            acc = pl.ds(pl.multiple_of(i * 128, 128), 128)
            by = slope[rows, 0:1] * math.sqrt(2.0)
            lat = jnp.sum(lat_acc[acc, :], axis=1, keepdims=True) * (scale * math.sqrt(2.0))
            thr = jnp.sum(thr_acc[acc, :], axis=1, keepdims=True) * scale * by
            grad = -(load_acc[acc, :] * (scale * by)) - (lat * by * by) * comp[rows, :].astype(F32)
            flat = grad.T
            for j in range(NSC):
                grads[j, :, rows] = flat[32 * j : 32 * (j + 1), :]
            thr_line[:, rows] = jnp.broadcast_to(thr, (128, 128)).T[0:1, :]

        run(0, count // 128, one)
        for k in (2, 1, 3, 0):
            pair_copy(c, k).start()
        thr_pair_copy(c).start()

    def pair_up(c):
        first, count = CHUNKS[c]
        at = pl.ds(first, count)
        for k in (2, 1, 3):
            pair_copy(c, k).wait_recv()
            sum_l[k, :, at] = (grads[((z + k) % 4) * 2 + core, :, at] + pair[k, :, at]).astype(BF)
            near_copy(c, k).start()
        thr_pair_copy(c).wait_recv()
        thr_sum[:, at] = thr_line[:, at] + thr_pair[:, at]
        for k in (2, 1, 3):
            thr_near_copy(c, k).start()
        pair_copy(c, 0).wait_recv()

    def near_up(c):
        first, count = CHUNKS[c]
        at = pl.ds(first, count)
        held = grads[sc, :, at] + pair[0, :, at]
        thr = thr_sum[:, at]
        for k in (1, 3, 2):
            near_copy(c, k).wait_recv()
            thr_near_copy(c, k).wait_recv()
            held = held + near_l[k, :, at].astype(F32)
            thr = thr + thr_near[k, :, at]
        for i in range(count // 128):
            part = slice(128 * i, 128 * (i + 1))
            full[first // 128 + i, 0:32, :] = held[:, part]
            full[first // 128 + i, 40:41, :] = thr[:, part]

    full[CAP // 128 :, :, :] = jnp.zeros((3, 48, 128), F32)
    full[0 : CAP // 128, 40:48, :] = jnp.zeros((CAP // 128, 8, 128), F32)
    steps = S // ST
    for c in range(len(CHUNKS)):
        load_acc[...] = jnp.zeros_like(load_acc)
        lat_acc[...] = jnp.zeros_like(lat_acc)
        thr_acc[...] = jnp.zeros_like(thr_acc)
        back_steps(c, 0, steps // 2)
        if c == 0:
            run(1, NSC, lambda k: date_out(k).wait_recv())
            line = dates[sc]
            for k in range(1, NSC):
                line = line + dates_in[k]
            date_sum[...] = line
            run(1, NSC, lambda k: date_share(k).start())
            date_all[sc] = line
        else:
            pair_up(c - 1)
        back_steps(c, steps // 2, steps)
        if c:
            near_up(c - 1)
        fold(c)
    last = len(CHUNKS) - 1
    run(1, NSC, lambda k: date_share(k).wait_recv())
    for j in range(NSC):
        for i in range(CAP // 128):
            full[i, 32 + j : 33 + j, :] = date_all[j, :, 128 * i : 128 * (i + 1)]
    pair_up(last)
    run(1, NSC, lambda k: (date_out(k).wait_send(), date_share(k).wait_send()))
    near_up(last)
    lane = lax.broadcasted_iota(jnp.int32, (48, SEG), 1)
    for block, (start, offset, live) in enumerate(places):
        tile = start >> 3
        piece = jnp.concatenate([full[tile], full[tile + 1], full[tile + 2]], axis=1)
        part = jnp.full((48, 384), start & 7, jnp.int32)
        for bit in (1, 2, 4):
            piece = jnp.where(part & bit != 0, pltpu.roll(piece, 384 - 16 * bit, 1), piece)
        row = (offset + 16 * (lane // 16)) * 16 + lane % 16
        pack[block] = jnp.where(row < live, piece[:, 0:SEG], 0.0).astype(BF)

    def back_copy(k):
        peer = (me + k) % NCP
        return remote(pack.at[peer], back.at[(me - peer + NCP) % NCP], sends_c.at[k], recvs_c.at[k], (peer, sc))

    run(1, NCP, lambda k: back_copy(k).start())
    back[0] = pack[me]
    for c in range(len(CHUNKS)):
        for k in range(4):
            pair_copy(c, k).wait_send()
        thr_pair_copy(c).wait_send()
        for k in range(1, 4):
            near_copy(c, k).wait_send()
            thr_near_copy(c, k).wait_send()
    run(1, NCP, lambda k: back_copy(k).wait_recv())
    group = lax.broadcasted_iota(jnp.int32, (48, 128), 1) // 16
    for g in range(2):
        for h in range(2):
            held = [back[8 * g + q, :, 128 * h : 128 * (h + 1)].astype(F32) for q in range(8)]
            for s in range(8):
                mixed = held[s]
                for q in range(8):
                    if q != s:
                        moved = pltpu.roll(held[q], (16 * (q - s)) % 128, 1)
                        mixed = jnp.where(group == q, moved, mixed)
                tile = 2 * (8 * h + s) + g
                at = slice(128 * tile, 128 * (tile + 1))
                load_out[:, at] = mixed[0:32, :]
                expo_out[:, at] = mixed[32:40, :]
                thr_out[:, at] = mixed[40:41, :]
    run(1, NCP, lambda k: back_copy(k).wait_send())


def main(tiles, expo_in, thr_in, factors, aversion, lengths):
    vmem = pl.BlockSpec(memory_space=pltpu.VMEM)
    dma = pltpu.SemaphoreType.DMA
    parts = len(CHUNKS)
    most = max(count for _, count in CHUNKS)
    return pl.pallas_call(
        main_kernel,
        out_shape=(
            jax.ShapeDtypeStruct((32, ROWS), F32),
            jax.ShapeDtypeStruct((1, ROWS), F32),
            jax.ShapeDtypeStruct((NSC, ROWS), F32),
            jax.ShapeDtypeStruct((8, 128), F32),
        ),
        in_specs=[pl.BlockSpec(memory_space=pl.ANY)] + [vmem] * 3 + [pl.BlockSpec(memory_space=pltpu.SMEM)] * 2,
        out_specs=[vmem] * 4,
        scratch_shapes=[
            pltpu.VMEM((NCP * 16, 16, F), BF),
            pltpu.VMEM((NCP, 16, SEG), BF),
            pltpu.VMEM((NCP, 16, SEG), BF),
            pltpu.VMEM((NCP * 16, 16, 128), F32),
            pltpu.VMEM((CAP, F), BF),
            pltpu.VMEM((CAP, 128), F32),
            pltpu.VMEM((CAP, 128), F32),
            pltpu.VMEM((CAP, 128), BF),
            pltpu.VMEM((16, CAP), BF),
            pltpu.SMEM((CAP // 16,), jnp.int32),
            pltpu.SMEM((CAP // 16,), jnp.int32),
            pltpu.VMEM((CAP // 128 + 3, 48, 128), F32),
            pltpu.VMEM((NCP, 48, SEG), BF),
            pltpu.VMEM((NCP, 48, SEG), BF),
            pltpu.VMEM((CAP, S), BF),
            pltpu.VMEM((8, S), F32),
            pltpu.VMEM((NCP, 8, S // NCP), F32),
            pltpu.VMEM((8, S // NCP), F32),
            pltpu.VMEM((8, S), F32),
            pltpu.VMEM((NSC, 16, 128), F32),
            pltpu.VMEM((16, S), BF),
            pltpu.VMEM((ST, 128), BF),
            pltpu.VMEM((CAP, 16), F32),
            pltpu.VMEM((NSC, 1, CAP), F32),
            pltpu.VMEM((NSC, 1, CAP), F32),
            pltpu.VMEM((1, CAP), F32),
            pltpu.VMEM((NSC, 1, CAP), F32),
            pltpu.VMEM((most, F), F32),
            pltpu.VMEM((most, 128), F32),
            pltpu.VMEM((most, 128), F32),
            pltpu.VMEM((NSC, 32, CAP), F32),
            pltpu.VMEM((4, 32, CAP), F32),
            pltpu.VMEM((4, 32, CAP), BF),
            pltpu.VMEM((4, 32, CAP), BF),
            pltpu.VMEM((1, CAP), F32),
            pltpu.VMEM((1, CAP), F32),
            pltpu.VMEM((1, CAP), F32),
            pltpu.VMEM((4, 1, CAP), F32),
            dma((NCP,)),
            dma((NCP,)),
            dma((NCP,)),
            dma((NCP,)),
            dma((NSC,)),
            dma((NSC,)),
            dma((NSC,)),
            dma((NSC,)),
            dma((NSC,)),
            dma((NSC,)),
            dma((parts, 5)),
            dma((parts, 5)),
            dma((parts, 4)),
            dma((parts, 4)),
            dma((parts, 4)),
            dma((parts, 4)),
            dma((NCP,)),
            dma((NCP,)),
            dma((NCP,)),
            dma((NCP,)),
            dma((NCP,)),
            dma((NCP,)),
            dma((NCP,)),
            dma((NCP,)),
            dma((1,)),
        ],
        compiler_params=pltpu.CompilerParams(
            collective_id=0, has_side_effects=True, vmem_limit_bytes=58 * 2**20
        ),
        name="main",
    )(tiles, expo_in, thr_in, factors, aversion, lengths)


def per_device(factors, loadings, thresholds, exposures, aversion, lengths):
    tiles = loadings.reshape(16, NCP, 16, F)
    load, thr, dates, risk = main(
        tiles, exposures.T, thresholds.reshape(1, ROWS), factors, aversion, lengths
    )
    return (load.T, thr.reshape(ROWS), dates.T, risk[:, 0])


def solution(mesh):
    in_specs = (P("sc", None), P("cp", None), P("cp"), P("cp", None), P(), P())
    out_specs = (P("cp", "sc"), P("cp"), P("cp", None), P())
    return jax.shard_map(
        per_device, mesh=mesh, in_specs=in_specs, out_specs=out_specs, check_vma=False
    )
```

```python
import math

import jax
import jax.numpy as jnp
from jax import lax
from jax.experimental import pallas as pl
from jax.experimental.pallas import tpu as pltpu
from jax.sharding import PartitionSpec as P

MESH = pl.DeviceIdType.MESH
NCP = 16
NSC = 8
F = 256
ROWS = 4096
S = 4096
CAP = 2176
SEG = ROWS // NCP
LIVE = 32768
SCEN = 32768
ST = 512
CHUNKS = ((0, 768), (768, 768), (1536, 640))
ROOT_HALF = 0.7071067811865476
LOG2E = 1.4426950408889634
FAR = -3.1
TAIL = (-0.750217616, 0.756257034, -1.37553279, 0.0025935648)
BF = jnp.bfloat16
F32 = jnp.float32


def spots(lengths_ref, position):
    low, high = [], []
    at = jnp.int32(0)
    beyond = jnp.int32(0)
    for block in range(NCP):
        offset = (position - block + NCP) % NCP
        tiles = (((lengths_ref[block] + 15) >> 4) - offset + 15) >> 4
        low.append(at)
        high.append(beyond)
        at = at + jnp.minimum(tiles, 8)
        beyond = beyond + jnp.maximum(tiles - 8, 0)
    return low, [at + place for place in high], at


def double_cdf(u):
    far = TAIL[3]
    for coef in TAIL[2::-1]:
        far = far * u + coef
    return jnp.where(u < FAR, jnp.exp2(far), 1.0 + lax.erf(u))


def run(first, last, act):
    def body(k, _):
        act(k)
        return 0

    lax.fori_loop(first, last, body, 0)


def main_kernel(
    tiles, expo_in, thr_in, factors, aversion, lengths, load_out, thr_out, expo_out, risk,
    got, got_high, small, got_small, wide, comp, shift, slope, expo, expo_t, table, lives, begins, full, pack, back, prob, loss, parts, mine, every, stats, weights, turned,
    expo_acc, dates, dates_in, date_sum, date_all,
    load_acc, lat_acc, thr_acc, grads, pair, sum_l, near_l, thr_line, thr_pair, thr_sum, thr_near,
    sends, recvs, sends_g, recvs_g, sends_z, recvs_z, sends_d, recvs_d, sends_e, recvs_e,
    sends_a, recvs_a, sends_b, recvs_b, sends_t, recvs_t, sends_c, recvs_c,
    sends_x, recvs_x, sends_s, recvs_s, sends_y, recvs_y, own,
):
    me = lax.axis_index("cp")
    sc = lax.axis_index("sc")
    core = sc % 2
    z = sc // 2
    sibling = sc + 1 - 2 * core
    width = S // NCP
    barrier = pltpu.get_barrier_semaphore()
    run(1, NCP, lambda k: pl.semaphore_signal(barrier, inc=1, device_id=((me + k) % NCP, sc), device_id_type=MESH))
    run(1, NSC, lambda k: pl.semaphore_signal(barrier, inc=1, device_id=(me, (sc + k) % NSC), device_id_type=MESH))

    def remote(src, dst, send, recv, to):
        return pltpu.make_async_remote_copy(
            src_ref=src, dst_ref=dst, send_sem=send, recv_sem=recv, device_id=to, device_id_type=MESH
        )

    half = core * 4

    def row_copy(k, high):
        peer = (me + k) % NCP
        return remote(
            tiles.at[pl.ds(8 * high + half, 4), (peer - me + NCP) % NCP],
            (got, got_high)[high].at[pl.ds(me * 8 + half, 4)],
            sends_x.at[high, k], recvs_x.at[high, k], (peer, sc),
        )

    def small_copy(k):
        peer = (me + k) % NCP
        return remote(
            small.at[(peer - me + NCP) % NCP], got_small.at[me], sends_s.at[k], recvs_s.at[k], (peer, sc)
        )

    def pass_on(k, high):
        at = pl.ds(((me - k + NCP) % NCP) * 8 + half, 4)
        part = (got, got_high)[high].at[at]
        return remote(part, part, sends_y.at[high, k], recvs_y.at[high, k], (me, sibling))

    def own_copy(high):
        return pltpu.make_async_copy(
            tiles.at[pl.ds(8 * high, 8), 0], (got, got_high)[high].at[pl.ds(me * 8, 8)], own.at[high]
        )

    chunk_of = lax.broadcasted_iota(jnp.int32, (16, 128), 1) // 16
    limits = jnp.broadcast_to(thr_in[...].astype(F32), (8, ROWS))
    raw = jnp.concatenate([expo_in[...].astype(F32), limits], axis=0)
    for t in range(NCP):
        for h in range(2):
            mixed = None
            for q in range(8):
                tile = 2 * (8 * h + q) + t // 8
                moved = pltpu.roll(raw[:, 128 * tile : 128 * (tile + 1)], (16 * (q - t % 8)) % 128, 1)
                mixed = moved if mixed is None else jnp.where(chunk_of == q, moved, mixed)
            small[t, :, 128 * h : 128 * (h + 1)] = mixed.astype(BF)

    pl.semaphore_wait(barrier, NCP + NSC - 2)
    run(1, NCP, lambda k: (small_copy(k).start(), row_copy(k, 0).start()))
    own_copy(0).start()
    run(1, NCP, lambda k: row_copy(k, 1).start())
    own_copy(1).start()
    got_small[me] = small[0]

    low, high, lows = spots(lengths, me)
    for block in range(NCP):
        begins[block] = low[block]
        begins[NCP + block] = high[block]

    def tabulate(k):
        block_low = jnp.int32(0)
        block_high = jnp.int32(0)
        for i in range(1, NCP):
            block_low = block_low + jnp.where(k >= begins[i], 1, 0)
            block_high = block_high + jnp.where(k >= begins[NCP + i], 1, 0)
        slot_low = jnp.clip(k - begins[block_low], 0, 7)
        past = k - begins[NCP + block_high]
        slot_high = jnp.clip(past, 0, 7)
        upper = k >= lows
        block = jnp.where(upper, block_high, block_low)
        slot = jnp.where(upper, slot_high + 8, slot_low)
        table[0, k] = block_low * 8 + slot_low
        table[1, k] = block_high * 8 + slot_high
        table[2, k] = block * 16 + slot
        table[3, k] = jnp.where(upper, 1, 0)
        offset = (me - block + NCP) & 15
        spare = jnp.where(upper & (past > 7), 32768, 0)
        lives[k] = lengths[block] - (offset + 16 * slot) * 16 - spare

    run(0, CAP // 16, tabulate)
    run(1, NCP, lambda k: small_copy(k).wait_recv())
    for block in range(NCP):
        part = got_small[block].astype(F32)
        part = jnp.concatenate([part, jnp.zeros((112, SEG), F32)], axis=0).T
        for slot in range(16):
            wide[block * 16 + slot] = part[16 * slot : 16 * (slot + 1), :]
    run(1, NCP, lambda k: (row_copy(k, 0).wait_recv(), pass_on(k, 0).start()))
    own_copy(0).wait()
    run(1, NCP, lambda k: pass_on(k, 0).wait_recv())

    row_of = lax.broadcasted_iota(jnp.int32, (16, 128), 0)
    lane_of = lax.broadcasted_iota(jnp.int32, (16, 128), 1)

    def compact(i, mixed):
        at = pl.ds(pl.multiple_of(i * 128, 128), 128)
        pieces = []
        for q in range(8):
            piece = got[table[0, 8 * i + q]].astype(F32)
            if mixed:
                upper = jnp.full((16, F), table[3, 8 * i + q], jnp.int32) > 0
                piece = jnp.where(upper, got_high[table[1, 8 * i + q]].astype(F32), piece)
            pieces.append(piece)
        rows = jnp.concatenate(pieces, axis=0)
        part = jnp.concatenate(
            [
                jnp.where((row_of < lives[8 * i + q]) | (lane_of >= 8), wide[table[2, 8 * i + q]], 0.0)
                for q in range(8)
            ],
            axis=0,
        )
        comp[at, :] = rows.astype(BF)
        total = jnp.sum(rows * rows, axis=1, keepdims=True)
        by = lax.rsqrt(1.0 + total) * ROOT_HALF
        slope[at, :] = jnp.broadcast_to(by, (128, 128))
        shift[at, :] = jnp.broadcast_to(part[:, 8:9] * by, (128, 128))
        expo[at, :] = part.astype(BF)
        expo_t[:, at] = part.T[0:16, :].astype(BF)

    def latent(first, count, cols):
        rows = pl.ds(first, count)
        project = lax.dot_general(
            comp[rows, :], factors[cols, :], (((1,), (1,)), ((), ())), preferred_element_type=F32
        )
        a = jnp.concatenate([shift[rows, :]] * (ST // 128), axis=1)
        b = jnp.concatenate([slope[rows, :]] * (ST // 128), axis=1)
        return a - project * b

    def ahead(step, parts_of):
        cols = pl.ds(pl.multiple_of(step * ST, ST), ST)
        for first, count in parts_of:
            prob[pl.ds(first, count), cols] = double_cdf(latent(first, count, cols)).astype(BF)

    def ahead_pass(step):
        ahead(step, CHUNKS[:1])
        for j in range(3):
            k = 1 + (step - 2) * 3 + j
            row_copy(k, 1).wait_recv()
            pass_on(k, 1).start()

    def ahead_rest(step):
        cols = pl.ds(pl.multiple_of(step * ST, ST), ST)
        ahead(step, CHUNKS[1:])
        loss[:, cols] = jnp.dot(expo_t[...], prob[:, cols], preferred_element_type=F32)[0:8, :]

    run(0, CHUNKS[0][1] // 128, lambda i: compact(i, False))
    run(0, 2, lambda step: ahead(step, CHUNKS[:1]))
    run(2, 7, ahead_pass)
    run(7, S // ST, lambda step: ahead(step, CHUNKS[:1]))
    own_copy(1).wait()
    run(1, NCP, lambda k: pass_on(k, 1).wait_recv())
    run(CHUNKS[0][1] // 128, CAP // 128, lambda i: compact(i, True))
    run(0, S // ST, ahead_rest)
    run(1, NCP, lambda k: (row_copy(k, 0).wait_send(), row_copy(k, 1).wait_send(), small_copy(k).wait_send()))
    run(1, NCP, lambda k: (pass_on(k, 0).wait_send(), pass_on(k, 1).wait_send()))

    def part_of(position):
        return pl.ds(pl.multiple_of(position * width, width), width)

    def scatter(k):
        peer = (me + k) % NCP
        return remote(loss.at[:, part_of(peer)], parts.at[me], sends.at[k], recvs.at[k], (peer, sc))

    def gather(k):
        return remote(mine, every.at[:, part_of(me)], sends_g.at[k], recvs_g.at[k], ((me + k) % NCP, sc))

    def share(k):
        return remote(stats.at[sc], stats.at[sc], sends_z.at[k], recvs_z.at[k], (me, (sc + k) % NSC))

    run(1, NCP, lambda k: scatter(k).start())
    parts[me] = loss[:, part_of(me)]
    at_date = lax.broadcasted_iota(jnp.int32, (8, 128), 0)
    averse = jnp.zeros((8, 128), F32)
    for t in range(8):
        averse = jnp.where(at_date == t, aversion[t], averse)
    run(1, NCP, lambda k: scatter(k).wait_recv())
    total = parts[0]
    for i in range(1, NCP):
        total = total + parts[i]
    score = jnp.concatenate([averse] * (width // 128), axis=1) * (total * (0.5 / LIVE))
    mine[...] = score
    run(1, NCP, lambda k: gather(k).start())
    every[:, part_of(me)] = score
    run(1, NCP, lambda k: gather(k).wait_recv())
    scores = every[...]
    top = jnp.max(scores, axis=1, keepdims=True)
    raised = jnp.exp(scores - top)
    mass = jnp.sum(raised, axis=1, keepdims=True)
    stats[sc, 0:8, :] = jnp.broadcast_to(top, (8, 128))
    stats[sc, 8:16, :] = jnp.broadcast_to(mass, (8, 128))
    run(1, NSC, lambda k: share(k).start())
    weights[...] = jnp.concatenate([raised, jnp.zeros((8, S), F32)], axis=0).astype(BF)

    expo_acc[...] = jnp.zeros_like(expo_acc)

    def expose(step):
        cols = pl.ds(pl.multiple_of(step * ST, ST), ST)
        turned[:, 0:16] = weights[:, cols].astype(F32).T.astype(BF)
        expo_acc[...] += jnp.dot(prob[:, cols], turned[:, 0:16], preferred_element_type=F32)

    run(0, S // ST, expose)
    run(1, NSC, lambda k: share(k).wait_recv())
    best = stats[0, 0:8, :]
    for i in range(1, NSC):
        best = jnp.maximum(best, stats[i, 0:8, :])
    heap = jnp.zeros((8, 128), F32)
    for i in range(NSC):
        heap = heap + stats[i, 8:16, :] * jnp.exp(stats[i, 0:8, :] - best)
    final = jnp.exp(every[...] - best[:, 0:1]) / heap[:, 0:1]
    weights[...] = jnp.concatenate([final, jnp.zeros((8, S), F32)], axis=0).astype(BF)
    risk[...] = (best + jnp.log(heap / SCEN)) / averse
    run(1, NCP, lambda k: scatter(k).wait_send())
    run(1, NCP, lambda k: gather(k).wait_send())
    run(1, NSC, lambda k: share(k).wait_send())
    own_scale = jnp.exp(stats[sc, 0:8, :] - best) / heap * (0.5 / LIVE)
    for i in range(CAP // 128):
        block = jnp.concatenate(
            [expo_acc[128 * i : 128 * (i + 1), :], jnp.zeros((128, 112), F32)], axis=1
        ).T
        for j in range(NSC):
            dates[j, :, 128 * i : 128 * (i + 1)] = block[j : j + 1, :] * own_scale[j : j + 1, :]

    def date_out(k):
        peer = (sc + k) % NSC
        return remote(dates.at[peer], dates_in.at[k], sends_d.at[k], recvs_d.at[k], (me, peer))

    def date_share(k):
        return remote(date_sum, date_all.at[sc], sends_e.at[k], recvs_e.at[k], (me, (sc + k) % NSC))

    run(1, NSC, lambda k: date_out(k).start())

    def pair_copy(c, k):
        first, count = CHUNKS[c]
        at = pl.ds(first, count)
        return remote(
            grads.at[((z + k) % 4) * 2 + 1 - core, :, at], pair.at[k, :, at],
            sends_a.at[c, k], recvs_a.at[c, k], (me, sibling),
        )

    def thr_pair_copy(c):
        at = pl.ds(*CHUNKS[c])
        return remote(thr_line.at[:, at], thr_pair.at[:, at], sends_a.at[c, 4], recvs_a.at[c, 4], (me, sibling))

    def near_copy(c, k):
        at = pl.ds(*CHUNKS[c])
        return remote(
            sum_l.at[k, :, at], near_l.at[k, :, at],
            sends_b.at[c, k], recvs_b.at[c, k], (me, ((z + k) % 4) * 2 + core),
        )

    def thr_near_copy(c, k):
        at = pl.ds(*CHUNKS[c])
        return remote(
            thr_sum.at[:, at], thr_near.at[k, :, at],
            sends_t.at[c, k], recvs_t.at[c, k], (me, ((z + k) % 4) * 2 + core),
        )

    def back_steps(c, low, high):
        first, count = CHUNKS[c]
        rows = pl.ds(first, count)
        acc = pl.ds(0, count)

        def step(i):
            cols = pl.ds(pl.multiple_of(i * ST, ST), ST)
            pull = jnp.dot(expo[rows, 0:16], weights[:, cols], preferred_element_type=F32)
            u = latent(first, count, cols)
            heavy = pull * jnp.exp2(u * u * (-LOG2E))
            lat = heavy * u
            lat_sum = lat[:, 0:128]
            thr_part = heavy[:, 0:128]
            for k in range(1, ST // 128):
                lat_sum = lat_sum + lat[:, k * 128 : (k + 1) * 128]
                thr_part = thr_part + heavy[:, k * 128 : (k + 1) * 128]
            lat_acc[acc, :] += lat_sum
            thr_acc[acc, :] += thr_part
            load_acc[acc, :] += jnp.dot(heavy.astype(BF), factors[cols, :], preferred_element_type=F32)

        run(low, high, step)

    def fold(c):
        first, count = CHUNKS[c]
        scale = 1.0 / (LIVE * math.sqrt(2.0 * math.pi))

        def one(i):
            rows = pl.ds(pl.multiple_of(first + i * 128, 128), 128)
            acc = pl.ds(pl.multiple_of(i * 128, 128), 128)
            by = slope[rows, 0:1] * math.sqrt(2.0)
            lat = jnp.sum(lat_acc[acc, :], axis=1, keepdims=True) * (scale * math.sqrt(2.0))
            thr = jnp.sum(thr_acc[acc, :], axis=1, keepdims=True) * scale * by
            grad = -(load_acc[acc, :] * (scale * by)) - (lat * by * by) * comp[rows, :].astype(F32)
            flat = grad.T
            for j in range(NSC):
                grads[j, :, rows] = flat[32 * j : 32 * (j + 1), :]
            thr_line[:, rows] = jnp.broadcast_to(thr, (128, 128)).T[0:1, :]

        run(0, count // 128, one)
        for k in (2, 1, 3, 0):
            pair_copy(c, k).start()
        thr_pair_copy(c).start()

    def pair_up(c):
        first, count = CHUNKS[c]
        at = pl.ds(first, count)
        for k in (2, 1, 3):
            pair_copy(c, k).wait_recv()
            sum_l[k, :, at] = (grads[((z + k) % 4) * 2 + core, :, at] + pair[k, :, at]).astype(BF)
            near_copy(c, k).start()
        thr_pair_copy(c).wait_recv()
        thr_sum[:, at] = thr_line[:, at] + thr_pair[:, at]
        for k in (2, 1, 3):
            thr_near_copy(c, k).start()
        pair_copy(c, 0).wait_recv()

    def near_up(c):
        first, count = CHUNKS[c]
        at = pl.ds(first, count)
        held = grads[sc, :, at] + pair[0, :, at]
        thr = thr_sum[:, at]
        for k in (1, 3, 2):
            near_copy(c, k).wait_recv()
            thr_near_copy(c, k).wait_recv()
            held = held + near_l[k, :, at].astype(F32)
            thr = thr + thr_near[k, :, at]
        for i in range(count // 128):
            part = slice(128 * i, 128 * (i + 1))
            full[first // 128 + i, 0:32, :] = held[:, part]
            full[first // 128 + i, 40:41, :] = thr[:, part]

    full[CAP // 128 :, :, :] = jnp.zeros((3, 48, 128), F32)
    full[0 : CAP // 128, 40:48, :] = jnp.zeros((CAP // 128, 8, 128), F32)
    steps = S // ST
    for c in range(len(CHUNKS)):
        load_acc[...] = jnp.zeros_like(load_acc)
        lat_acc[...] = jnp.zeros_like(lat_acc)
        thr_acc[...] = jnp.zeros_like(thr_acc)
        back_steps(c, 0, steps // 2)
        if c == 0:
            run(1, NSC, lambda k: date_out(k).wait_recv())
            line = dates[sc]
            for k in range(1, NSC):
                line = line + dates_in[k]
            date_sum[...] = line
            run(1, NSC, lambda k: date_share(k).start())
            date_all[sc] = line
        else:
            pair_up(c - 1)
        back_steps(c, steps // 2, steps)
        if c:
            near_up(c - 1)
        fold(c)
    last = len(CHUNKS) - 1
    run(1, NSC, lambda k: date_share(k).wait_recv())
    for j in range(NSC):
        for i in range(CAP // 128):
            full[i, 32 + j : 33 + j, :] = date_all[j, :, 128 * i : 128 * (i + 1)]
    pair_up(last)
    run(1, NSC, lambda k: (date_out(k).wait_send(), date_share(k).wait_send()))
    near_up(last)
    lane = lax.broadcasted_iota(jnp.int32, (48, 128), 1)
    for block in range(NCP):
        offset = (me - block + NCP) % NCP
        for upper, start in ((0, low[block]), (1, high[block])):
            tile = start >> 3
            piece = jnp.concatenate([full[tile], full[tile + 1]], axis=1)
            part = jnp.full((48, 256), start & 7, jnp.int32)
            for bit in (1, 2, 4):
                piece = jnp.where(part & bit != 0, pltpu.roll(piece, 256 - 16 * bit, 1), piece)
            row = (offset + 16 * (8 * upper + lane // 16)) * 16 + lane % 16
            pack[block, :, 128 * upper : 128 * (upper + 1)] = jnp.where(
                row < lengths[block], piece[:, 0:128], 0.0
            ).astype(BF)

    def back_copy(k):
        peer = (me + k) % NCP
        return remote(pack.at[peer], back.at[(me - peer + NCP) % NCP], sends_c.at[k], recvs_c.at[k], (peer, sc))

    run(1, NCP, lambda k: back_copy(k).start())
    back[0] = pack[me]
    for c in range(len(CHUNKS)):
        for k in range(4):
            pair_copy(c, k).wait_send()
        thr_pair_copy(c).wait_send()
        for k in range(1, 4):
            near_copy(c, k).wait_send()
            thr_near_copy(c, k).wait_send()
    run(1, NCP, lambda k: back_copy(k).wait_recv())
    group = lax.broadcasted_iota(jnp.int32, (48, 128), 1) // 16
    for g in range(2):
        for h in range(2):
            held = [back[8 * g + q, :, 128 * h : 128 * (h + 1)].astype(F32) for q in range(8)]
            for s in range(8):
                mixed = held[s]
                for q in range(8):
                    if q != s:
                        moved = pltpu.roll(held[q], (16 * (q - s)) % 128, 1)
                        mixed = jnp.where(group == q, moved, mixed)
                tile = 2 * (8 * h + s) + g
                at = slice(128 * tile, 128 * (tile + 1))
                load_out[:, at] = mixed[0:32, :]
                expo_out[:, at] = mixed[32:40, :]
                thr_out[:, at] = mixed[40:41, :]
    run(1, NCP, lambda k: back_copy(k).wait_send())


def main(tiles, expo_in, thr_in, factors, aversion, lengths):
    vmem = pl.BlockSpec(memory_space=pltpu.VMEM)
    dma = pltpu.SemaphoreType.DMA
    parts = len(CHUNKS)
    most = max(count for _, count in CHUNKS)
    return pl.pallas_call(
        main_kernel,
        out_shape=(
            jax.ShapeDtypeStruct((32, ROWS), F32),
            jax.ShapeDtypeStruct((1, ROWS), F32),
            jax.ShapeDtypeStruct((NSC, ROWS), F32),
            jax.ShapeDtypeStruct((8, 128), F32),
        ),
        in_specs=[pl.BlockSpec(memory_space=pl.ANY)] + [vmem] * 3 + [pl.BlockSpec(memory_space=pltpu.SMEM)] * 2,
        out_specs=[vmem] * 4,
        scratch_shapes=[
            pltpu.VMEM((NCP * 8, 16, F), BF),
            pltpu.VMEM((NCP * 8, 16, F), BF),
            pltpu.VMEM((NCP, 16, SEG), BF),
            pltpu.VMEM((NCP, 16, SEG), BF),
            pltpu.VMEM((NCP * 16, 16, 128), F32),
            pltpu.VMEM((CAP, F), BF),
            pltpu.VMEM((CAP, 128), F32),
            pltpu.VMEM((CAP, 128), F32),
            pltpu.VMEM((CAP, 128), BF),
            pltpu.VMEM((16, CAP), BF),
            pltpu.SMEM((4, CAP // 16), jnp.int32),
            pltpu.SMEM((CAP // 16,), jnp.int32),
            pltpu.SMEM((2 * NCP,), jnp.int32),
            pltpu.VMEM((CAP // 128 + 3, 48, 128), F32),
            pltpu.VMEM((NCP, 48, SEG), BF),
            pltpu.VMEM((NCP, 48, SEG), BF),
            pltpu.VMEM((CAP, S), BF),
            pltpu.VMEM((8, S), F32),
            pltpu.VMEM((NCP, 8, S // NCP), F32),
            pltpu.VMEM((8, S // NCP), F32),
            pltpu.VMEM((8, S), F32),
            pltpu.VMEM((NSC, 16, 128), F32),
            pltpu.VMEM((16, S), BF),
            pltpu.VMEM((ST, 128), BF),
            pltpu.VMEM((CAP, 16), F32),
            pltpu.VMEM((NSC, 1, CAP), F32),
            pltpu.VMEM((NSC, 1, CAP), F32),
            pltpu.VMEM((1, CAP), F32),
            pltpu.VMEM((NSC, 1, CAP), F32),
            pltpu.VMEM((most, F), F32),
            pltpu.VMEM((most, 128), F32),
            pltpu.VMEM((most, 128), F32),
            pltpu.VMEM((NSC, 32, CAP), F32),
            pltpu.VMEM((4, 32, CAP), F32),
            pltpu.VMEM((4, 32, CAP), BF),
            pltpu.VMEM((4, 32, CAP), BF),
            pltpu.VMEM((1, CAP), F32),
            pltpu.VMEM((1, CAP), F32),
            pltpu.VMEM((1, CAP), F32),
            pltpu.VMEM((4, 1, CAP), F32),
            dma((NCP,)),
            dma((NCP,)),
            dma((NCP,)),
            dma((NCP,)),
            dma((NSC,)),
            dma((NSC,)),
            dma((NSC,)),
            dma((NSC,)),
            dma((NSC,)),
            dma((NSC,)),
            dma((parts, 5)),
            dma((parts, 5)),
            dma((parts, 4)),
            dma((parts, 4)),
            dma((parts, 4)),
            dma((parts, 4)),
            dma((NCP,)),
            dma((NCP,)),
            dma((2, NCP)),
            dma((2, NCP)),
            dma((NCP,)),
            dma((NCP,)),
            dma((2, NCP)),
            dma((2, NCP)),
            dma((2,)),
        ],
        compiler_params=pltpu.CompilerParams(
            collective_id=0, has_side_effects=True, vmem_limit_bytes=58 * 2**20
        ),
        name="main",
    )(tiles, expo_in, thr_in, factors, aversion, lengths)


def per_device(factors, loadings, thresholds, exposures, aversion, lengths):
    tiles = loadings.reshape(16, NCP, 16, F)
    load, thr, dates, risk = main(
        tiles, exposures.T, thresholds.reshape(1, ROWS), factors, aversion, lengths
    )
    return (load.T, thr.reshape(ROWS), dates.T, risk[:, 0])


def solution(mesh):
    in_specs = (P("sc", None), P("cp", None), P("cp"), P("cp", None), P(), P())
    out_specs = (P("cp", "sc"), P("cp"), P("cp", None), P())
    return jax.shard_map(
        per_device, mesh=mesh, in_specs=in_specs, out_specs=out_specs, check_vma=False
    )
```

```python
import math

import jax
import jax.numpy as jnp
from jax import lax
from jax.experimental import pallas as pl
from jax.experimental.pallas import tpu as pltpu
from jax.sharding import PartitionSpec as P

MESH = pl.DeviceIdType.MESH
NCP = 16
NSC = 8
F = 256
ROWS = 4096
S = 4096
CAP = 2176
SEG = ROWS // NCP
LIVE = 32768
SCEN = 32768
ST = 512
CHUNKS = ((0, 896), (896, 768), (1664, 512))
ROOT_HALF = 0.7071067811865476
LOG2E = 1.4426950408889634
FAR = -3.1
TAIL = (-0.750217616, 0.756257034, -1.37553279, 0.0025935648)
KEPT = 1
BF = jnp.bfloat16
F32 = jnp.float32


def spots(lengths_ref, position):
    low, high = [], []
    at = jnp.int32(0)
    beyond = jnp.int32(0)
    for block in range(NCP):
        offset = (position - block + NCP) % NCP
        tiles = (((lengths_ref[block] + 15) >> 4) - offset + 15) >> 4
        low.append(at)
        high.append(beyond)
        at = at + jnp.minimum(tiles, 8)
        beyond = beyond + jnp.maximum(tiles - 8, 0)
    return low, [at + place for place in high], at


def double_cdf(u):
    far = TAIL[3]
    for coef in TAIL[2::-1]:
        far = far * u + coef
    return jnp.where(u < FAR, jnp.exp2(far), 1.0 + lax.erf(u))


def run(first, last, act):
    def body(k, _):
        act(k)
        return 0

    lax.fori_loop(first, last, body, 0)


def main_kernel(
    tiles, expo_in, thr_in, factors, aversion, lengths, load_out, thr_out, expo_out, risk,
    got, got_high, small, got_small, wide, comp, shift, slope, expo, expo_t, table, lives, begins, kept, full, pack, back, prob, loss, parts, mine, every, stats, weights, turned,
    expo_acc, dates, dates_in, date_sum, date_all,
    load_acc, lat_acc, thr_acc, grads, pair, sum_l, near_l, thr_line, thr_pair, thr_sum, thr_near,
    sends, recvs, sends_g, recvs_g, sends_z, recvs_z, sends_d, recvs_d, sends_e, recvs_e,
    sends_a, recvs_a, sends_b, recvs_b, sends_t, recvs_t, sends_c, recvs_c,
    sends_x, recvs_x, sends_s, recvs_s, sends_y, recvs_y, own,
):
    me = lax.axis_index("cp")
    sc = lax.axis_index("sc")
    core = sc % 2
    z = sc // 2
    sibling = sc + 1 - 2 * core
    width = S // NCP
    barrier = pltpu.get_barrier_semaphore()
    run(1, NCP, lambda k: pl.semaphore_signal(barrier, inc=1, device_id=((me + k) % NCP, sc), device_id_type=MESH))
    run(1, NSC, lambda k: pl.semaphore_signal(barrier, inc=1, device_id=(me, (sc + k) % NSC), device_id_type=MESH))

    def remote(src, dst, send, recv, to):
        return pltpu.make_async_remote_copy(
            src_ref=src, dst_ref=dst, send_sem=send, recv_sem=recv, device_id=to, device_id_type=MESH
        )

    half = core * 4

    def row_copy(k, high):
        peer = (me + k) % NCP
        return remote(
            tiles.at[pl.ds(8 * high + half, 4), (peer - me + NCP) % NCP],
            (got, got_high)[high].at[pl.ds(me * 8 + half, 4)],
            sends_x.at[high, k], recvs_x.at[high, k], (peer, sc),
        )

    def small_copy(k):
        peer = (me + k) % NCP
        return remote(
            small.at[(peer - me + NCP) % NCP], got_small.at[me], sends_s.at[k], recvs_s.at[k], (peer, sc)
        )

    def pass_on(k, high):
        at = pl.ds(((me - k + NCP) % NCP) * 8 + half, 4)
        part = (got, got_high)[high].at[at]
        return remote(part, part, sends_y.at[high, k], recvs_y.at[high, k], (me, sibling))

    def own_copy(high):
        return pltpu.make_async_copy(
            tiles.at[pl.ds(8 * high, 8), 0], (got, got_high)[high].at[pl.ds(me * 8, 8)], own.at[high]
        )

    chunk_of = lax.broadcasted_iota(jnp.int32, (16, 128), 1) // 16
    limits = jnp.broadcast_to(thr_in[...].astype(F32), (8, ROWS))
    raw = jnp.concatenate([expo_in[...].astype(F32), limits], axis=0)
    for t in range(NCP):
        for h in range(2):
            mixed = None
            for q in range(8):
                tile = 2 * (8 * h + q) + t // 8
                moved = pltpu.roll(raw[:, 128 * tile : 128 * (tile + 1)], (16 * (q - t % 8)) % 128, 1)
                mixed = moved if mixed is None else jnp.where(chunk_of == q, moved, mixed)
            small[t, :, 128 * h : 128 * (h + 1)] = mixed.astype(BF)

    pl.semaphore_wait(barrier, NCP + NSC - 2)
    run(1, NCP, lambda k: (small_copy(k).start(), row_copy(k, 0).start()))
    own_copy(0).start()
    run(1, NCP, lambda k: row_copy(k, 1).start())
    own_copy(1).start()
    got_small[me] = small[0]

    low, high, lows = spots(lengths, me)
    for block in range(NCP):
        begins[block] = low[block]
        begins[NCP + block] = high[block]

    def tabulate(k):
        block_low = jnp.int32(0)
        block_high = jnp.int32(0)
        for i in range(1, NCP):
            block_low = block_low + jnp.where(k >= begins[i], 1, 0)
            block_high = block_high + jnp.where(k >= begins[NCP + i], 1, 0)
        slot_low = jnp.clip(k - begins[block_low], 0, 7)
        past = k - begins[NCP + block_high]
        slot_high = jnp.clip(past, 0, 7)
        upper = k >= lows
        block = jnp.where(upper, block_high, block_low)
        slot = jnp.where(upper, slot_high + 8, slot_low)
        table[0, k] = block_low * 8 + slot_low
        table[1, k] = block_high * 8 + slot_high
        table[2, k] = block * 16 + slot
        table[3, k] = jnp.where(upper, 1, 0)
        offset = (me - block + NCP) & 15
        spare = jnp.where(upper & (past > 7), 32768, 0)
        lives[k] = lengths[block] - (offset + 16 * slot) * 16 - spare

    run(0, CAP // 16, tabulate)
    run(1, NCP, lambda k: small_copy(k).wait_recv())
    for block in range(NCP):
        part = got_small[block].astype(F32)
        part = jnp.concatenate([part, jnp.zeros((112, SEG), F32)], axis=0).T
        for slot in range(16):
            wide[block * 16 + slot] = part[16 * slot : 16 * (slot + 1), :]
    run(1, NCP, lambda k: (row_copy(k, 0).wait_recv(), pass_on(k, 0).start()))
    own_copy(0).wait()
    run(1, NCP, lambda k: pass_on(k, 0).wait_recv())

    row_of = lax.broadcasted_iota(jnp.int32, (16, 128), 0)
    lane_of = lax.broadcasted_iota(jnp.int32, (16, 128), 1)

    def compact(i, mixed):
        at = pl.ds(pl.multiple_of(i * 128, 128), 128)
        pieces = []
        for q in range(8):
            piece = got[table[0, 8 * i + q]].astype(F32)
            if mixed:
                upper = jnp.full((16, F), table[3, 8 * i + q], jnp.int32) > 0
                piece = jnp.where(upper, got_high[table[1, 8 * i + q]].astype(F32), piece)
            pieces.append(piece)
        rows = jnp.concatenate(pieces, axis=0)
        part = jnp.concatenate(
            [
                jnp.where((row_of < lives[8 * i + q]) | (lane_of >= 8), wide[table[2, 8 * i + q]], 0.0)
                for q in range(8)
            ],
            axis=0,
        )
        comp[at, :] = rows.astype(BF)
        total = jnp.sum(rows * rows, axis=1, keepdims=True)
        by = lax.rsqrt(1.0 + total) * ROOT_HALF
        slope[at, :] = jnp.broadcast_to(by, (128, 128))
        shift[at, :] = jnp.broadcast_to(part[:, 8:9] * by, (128, 128))
        expo[at, :] = part.astype(BF)
        expo_t[:, at] = part.T[0:16, :].astype(BF)

    def latent(first, count, cols):
        rows = pl.ds(first, count)
        project = lax.dot_general(
            comp[rows, :], factors[cols, :], (((1,), (1,)), ((), ())), preferred_element_type=F32
        )
        a = jnp.concatenate([shift[rows, :]] * (ST // 128), axis=1)
        b = jnp.concatenate([slope[rows, :]] * (ST // 128), axis=1)
        return a - project * b

    def ahead(step, parts_of):
        cols = pl.ds(pl.multiple_of(step * ST, ST), ST)
        for first, count in parts_of:
            u = latent(first, count, cols)
            if (first, count) == CHUNKS[KEPT]:
                kept[:, cols] = u
            prob[pl.ds(first, count), cols] = double_cdf(u).astype(BF)

    def ahead_pass(step):
        ahead(step, CHUNKS[:1])
        for j in range(3):
            k = 1 + (step - 2) * 3 + j
            row_copy(k, 1).wait_recv()
            pass_on(k, 1).start()

    def ahead_rest(step):
        cols = pl.ds(pl.multiple_of(step * ST, ST), ST)
        ahead(step, CHUNKS[1:])
        loss[:, cols] = jnp.dot(expo_t[...], prob[:, cols], preferred_element_type=F32)[0:8, :]

    run(0, CHUNKS[0][1] // 128, lambda i: compact(i, False))
    run(0, 2, lambda step: ahead(step, CHUNKS[:1]))
    run(2, 7, ahead_pass)
    run(7, S // ST, lambda step: ahead(step, CHUNKS[:1]))
    own_copy(1).wait()
    run(1, NCP, lambda k: pass_on(k, 1).wait_recv())
    run(CHUNKS[0][1] // 128, CAP // 128, lambda i: compact(i, True))
    run(0, S // ST, ahead_rest)
    run(1, NCP, lambda k: (row_copy(k, 0).wait_send(), row_copy(k, 1).wait_send(), small_copy(k).wait_send()))
    run(1, NCP, lambda k: (pass_on(k, 0).wait_send(), pass_on(k, 1).wait_send()))

    def part_of(position):
        return pl.ds(pl.multiple_of(position * width, width), width)

    def scatter(k):
        peer = (me + k) % NCP
        return remote(loss.at[:, part_of(peer)], parts.at[me], sends.at[k], recvs.at[k], (peer, sc))

    def gather(k):
        return remote(mine, every.at[:, part_of(me)], sends_g.at[k], recvs_g.at[k], ((me + k) % NCP, sc))

    def share(k):
        return remote(stats.at[sc], stats.at[sc], sends_z.at[k], recvs_z.at[k], (me, (sc + k) % NSC))

    run(1, NCP, lambda k: scatter(k).start())
    parts[me] = loss[:, part_of(me)]
    at_date = lax.broadcasted_iota(jnp.int32, (8, 128), 0)
    averse = jnp.zeros((8, 128), F32)
    for t in range(8):
        averse = jnp.where(at_date == t, aversion[t], averse)
    run(1, NCP, lambda k: scatter(k).wait_recv())
    total = parts[0]
    for i in range(1, NCP):
        total = total + parts[i]
    score = jnp.concatenate([averse] * (width // 128), axis=1) * (total * (0.5 / LIVE))
    mine[...] = score
    run(1, NCP, lambda k: gather(k).start())
    every[:, part_of(me)] = score
    run(1, NCP, lambda k: gather(k).wait_recv())
    scores = every[...]
    top = jnp.max(scores, axis=1, keepdims=True)
    raised = jnp.exp(scores - top)
    mass = jnp.sum(raised, axis=1, keepdims=True)
    stats[sc, 0:8, :] = jnp.broadcast_to(top, (8, 128))
    stats[sc, 8:16, :] = jnp.broadcast_to(mass, (8, 128))
    run(1, NSC, lambda k: share(k).start())
    weights[...] = jnp.concatenate([raised, jnp.zeros((8, S), F32)], axis=0).astype(BF)

    expo_acc[...] = jnp.zeros_like(expo_acc)

    def expose(step):
        cols = pl.ds(pl.multiple_of(step * ST, ST), ST)
        turned[:, 0:16] = weights[:, cols].astype(F32).T.astype(BF)
        expo_acc[...] += jnp.dot(prob[:, cols], turned[:, 0:16], preferred_element_type=F32)

    run(0, S // ST, expose)
    run(1, NSC, lambda k: share(k).wait_recv())
    best = stats[0, 0:8, :]
    for i in range(1, NSC):
        best = jnp.maximum(best, stats[i, 0:8, :])
    heap = jnp.zeros((8, 128), F32)
    for i in range(NSC):
        heap = heap + stats[i, 8:16, :] * jnp.exp(stats[i, 0:8, :] - best)
    final = jnp.exp(every[...] - best[:, 0:1]) / heap[:, 0:1]
    weights[...] = jnp.concatenate([final, jnp.zeros((8, S), F32)], axis=0).astype(BF)
    risk[...] = (best + jnp.log(heap / SCEN)) / averse
    run(1, NCP, lambda k: scatter(k).wait_send())
    run(1, NCP, lambda k: gather(k).wait_send())
    run(1, NSC, lambda k: share(k).wait_send())
    own_scale = jnp.exp(stats[sc, 0:8, :] - best) / heap * (0.5 / LIVE)
    for i in range(CAP // 128):
        block = jnp.concatenate(
            [expo_acc[128 * i : 128 * (i + 1), :], jnp.zeros((128, 112), F32)], axis=1
        ).T
        for j in range(NSC):
            dates[j, :, 128 * i : 128 * (i + 1)] = block[j : j + 1, :] * own_scale[j : j + 1, :]

    def date_out(k):
        peer = (sc + k) % NSC
        return remote(dates.at[peer], dates_in.at[k], sends_d.at[k], recvs_d.at[k], (me, peer))

    def date_share(k):
        return remote(date_sum, date_all.at[sc], sends_e.at[k], recvs_e.at[k], (me, (sc + k) % NSC))

    run(1, NSC, lambda k: date_out(k).start())

    def pair_copy(c, k):
        first, count = CHUNKS[c]
        at = pl.ds(first, count)
        return remote(
            grads.at[((z + k) % 4) * 2 + 1 - core, :, at], pair.at[k, :, at],
            sends_a.at[c, k], recvs_a.at[c, k], (me, sibling),
        )

    def thr_pair_copy(c):
        at = pl.ds(*CHUNKS[c])
        return remote(thr_line.at[:, at], thr_pair.at[:, at], sends_a.at[c, 4], recvs_a.at[c, 4], (me, sibling))

    def near_copy(c, k):
        at = pl.ds(*CHUNKS[c])
        return remote(
            sum_l.at[k, :, at], near_l.at[k, :, at],
            sends_b.at[c, k], recvs_b.at[c, k], (me, ((z + k) % 4) * 2 + core),
        )

    def thr_near_copy(c, k):
        at = pl.ds(*CHUNKS[c])
        return remote(
            thr_sum.at[:, at], thr_near.at[k, :, at],
            sends_t.at[c, k], recvs_t.at[c, k], (me, ((z + k) % 4) * 2 + core),
        )

    def back_steps(c, low, high):
        first, count = CHUNKS[c]
        rows = pl.ds(first, count)
        acc = pl.ds(0, count)

        def step(i):
            cols = pl.ds(pl.multiple_of(i * ST, ST), ST)
            pull = jnp.dot(expo[rows, 0:16], weights[:, cols], preferred_element_type=F32)
            u = kept[:, cols] if c == KEPT else latent(first, count, cols)
            heavy = pull * jnp.exp2(u * u * (-LOG2E))
            lat = heavy * u
            lat_sum = lat[:, 0:128]
            thr_part = heavy[:, 0:128]
            for k in range(1, ST // 128):
                lat_sum = lat_sum + lat[:, k * 128 : (k + 1) * 128]
                thr_part = thr_part + heavy[:, k * 128 : (k + 1) * 128]
            lat_acc[acc, :] += lat_sum
            thr_acc[acc, :] += thr_part
            load_acc[acc, :] += jnp.dot(heavy.astype(BF), factors[cols, :], preferred_element_type=F32)

        run(low, high, step)

    def fold(c):
        first, count = CHUNKS[c]
        scale = 1.0 / (LIVE * math.sqrt(2.0 * math.pi))

        def one(i):
            rows = pl.ds(pl.multiple_of(first + i * 128, 128), 128)
            acc = pl.ds(pl.multiple_of(i * 128, 128), 128)
            by = slope[rows, 0:1] * math.sqrt(2.0)
            lat = jnp.sum(lat_acc[acc, :], axis=1, keepdims=True) * (scale * math.sqrt(2.0))
            thr = jnp.sum((thr_acc[acc, :] * (scale * by)).T, axis=0, keepdims=True)
            grad = -(load_acc[acc, :] * (scale * by)) - (lat * by * by) * comp[rows, :].astype(F32)
            flat = grad.T
            for j in range(NSC):
                grads[j, :, rows] = flat[32 * j : 32 * (j + 1), :]
            thr_line[:, rows] = thr

        run(0, count // 128, one)
        for k in (2, 1, 3, 0):
            pair_copy(c, k).start()
        thr_pair_copy(c).start()

    def pair_up(c):
        first, count = CHUNKS[c]
        at = pl.ds(first, count)
        for k in (2, 1, 3):
            pair_copy(c, k).wait_recv()
            sum_l[k, :, at] = (grads[((z + k) % 4) * 2 + core, :, at] + pair[k, :, at]).astype(BF)
            near_copy(c, k).start()
        thr_pair_copy(c).wait_recv()
        thr_sum[:, at] = thr_line[:, at] + thr_pair[:, at]
        for k in (2, 1, 3):
            thr_near_copy(c, k).start()
        pair_copy(c, 0).wait_recv()

    def near_up(c):
        first, count = CHUNKS[c]
        at = pl.ds(first, count)
        held = grads[sc, :, at] + pair[0, :, at]
        thr = thr_sum[:, at]
        for k in (1, 3, 2):
            near_copy(c, k).wait_recv()
            thr_near_copy(c, k).wait_recv()
            held = held + near_l[k, :, at].astype(F32)
            thr = thr + thr_near[k, :, at]
        for i in range(count // 128):
            part = slice(128 * i, 128 * (i + 1))
            full[first // 128 + i, 0:32, :] = held[:, part]
            full[first // 128 + i, 40:41, :] = thr[:, part]

    full[CAP // 128 :, :, :] = jnp.zeros((3, 48, 128), F32)
    full[0 : CAP // 128, 40:48, :] = jnp.zeros((CAP // 128, 8, 128), F32)
    steps = S // ST
    for c in range(len(CHUNKS)):
        load_acc[...] = jnp.zeros_like(load_acc)
        lat_acc[...] = jnp.zeros_like(lat_acc)
        thr_acc[...] = jnp.zeros_like(thr_acc)
        back_steps(c, 0, steps // 2)
        if c == 0:
            run(1, NSC, lambda k: date_out(k).wait_recv())
            line = dates[sc]
            for k in range(1, NSC):
                line = line + dates_in[k]
            date_sum[...] = line
            run(1, NSC, lambda k: date_share(k).start())
            date_all[sc] = line
        else:
            pair_up(c - 1)
        back_steps(c, steps // 2, steps)
        if c:
            near_up(c - 1)
        fold(c)
    last = len(CHUNKS) - 1
    run(1, NSC, lambda k: date_share(k).wait_recv())
    for j in range(NSC):
        for i in range(CAP // 128):
            full[i, 32 + j : 33 + j, :] = date_all[j, :, 128 * i : 128 * (i + 1)]
    pair_up(last)
    run(1, NSC, lambda k: (date_out(k).wait_send(), date_share(k).wait_send()))
    near_up(last)
    lane = lax.broadcasted_iota(jnp.int32, (48, 128), 1)
    for block in range(NCP):
        offset = (me - block + NCP) % NCP
        for upper, start in ((0, low[block]), (1, high[block])):
            tile = start >> 3
            piece = jnp.concatenate([full[tile], full[tile + 1]], axis=1)
            part = jnp.full((48, 256), start & 7, jnp.int32)
            for bit in (1, 2, 4):
                piece = jnp.where(part & bit != 0, pltpu.roll(piece, 256 - 16 * bit, 1), piece)
            row = (offset + 16 * (8 * upper + lane // 16)) * 16 + lane % 16
            pack[block, :, 128 * upper : 128 * (upper + 1)] = jnp.where(
                row < lengths[block], piece[:, 0:128], 0.0
            ).astype(BF)

    def back_copy(k):
        peer = (me + k) % NCP
        return remote(pack.at[peer], back.at[(me - peer + NCP) % NCP], sends_c.at[k], recvs_c.at[k], (peer, sc))

    run(1, NCP, lambda k: back_copy(k).start())
    back[0] = pack[me]
    for c in range(len(CHUNKS)):
        for k in range(4):
            pair_copy(c, k).wait_send()
        thr_pair_copy(c).wait_send()
        for k in range(1, 4):
            near_copy(c, k).wait_send()
            thr_near_copy(c, k).wait_send()
    run(1, NCP, lambda k: back_copy(k).wait_recv())
    group = lax.broadcasted_iota(jnp.int32, (48, 128), 1) // 16
    for g in range(2):
        for h in range(2):
            held = [back[8 * g + q, :, 128 * h : 128 * (h + 1)].astype(F32) for q in range(8)]
            for s in range(8):
                mixed = held[s]
                for q in range(8):
                    if q != s:
                        moved = pltpu.roll(held[q], (16 * (q - s)) % 128, 1)
                        mixed = jnp.where(group == q, moved, mixed)
                tile = 2 * (8 * h + s) + g
                at = slice(128 * tile, 128 * (tile + 1))
                load_out[:, at] = mixed[0:32, :]
                expo_out[:, at] = mixed[32:40, :]
                thr_out[:, at] = mixed[40:41, :]
    run(1, NCP, lambda k: back_copy(k).wait_send())


def main(tiles, expo_in, thr_in, factors, aversion, lengths):
    vmem = pl.BlockSpec(memory_space=pltpu.VMEM)
    dma = pltpu.SemaphoreType.DMA
    parts = len(CHUNKS)
    most = max(count for _, count in CHUNKS)
    return pl.pallas_call(
        main_kernel,
        out_shape=(
            jax.ShapeDtypeStruct((32, ROWS), F32),
            jax.ShapeDtypeStruct((1, ROWS), F32),
            jax.ShapeDtypeStruct((NSC, ROWS), F32),
            jax.ShapeDtypeStruct((8, 128), F32),
        ),
        in_specs=[pl.BlockSpec(memory_space=pl.ANY)] + [vmem] * 3 + [pl.BlockSpec(memory_space=pltpu.SMEM)] * 2,
        out_specs=[vmem] * 4,
        scratch_shapes=[
            pltpu.VMEM((NCP * 8, 16, F), BF),
            pltpu.VMEM((NCP * 8, 16, F), BF),
            pltpu.VMEM((NCP, 16, SEG), BF),
            pltpu.VMEM((NCP, 16, SEG), BF),
            pltpu.VMEM((NCP * 16, 16, 128), F32),
            pltpu.VMEM((CAP, F), BF),
            pltpu.VMEM((CAP, 128), F32),
            pltpu.VMEM((CAP, 128), F32),
            pltpu.VMEM((CAP, 128), BF),
            pltpu.VMEM((16, CAP), BF),
            pltpu.SMEM((4, CAP // 16), jnp.int32),
            pltpu.SMEM((CAP // 16,), jnp.int32),
            pltpu.SMEM((2 * NCP,), jnp.int32),
            pltpu.VMEM((CHUNKS[KEPT][1], S), F32),
            pltpu.VMEM((CAP // 128 + 3, 48, 128), F32),
            pltpu.VMEM((NCP, 48, SEG), BF),
            pltpu.VMEM((NCP, 48, SEG), BF),
            pltpu.VMEM((CAP, S), BF),
            pltpu.VMEM((8, S), F32),
            pltpu.VMEM((NCP, 8, S // NCP), F32),
            pltpu.VMEM((8, S // NCP), F32),
            pltpu.VMEM((8, S), F32),
            pltpu.VMEM((NSC, 16, 128), F32),
            pltpu.VMEM((16, S), BF),
            pltpu.VMEM((ST, 128), BF),
            pltpu.VMEM((CAP, 16), F32),
            pltpu.VMEM((NSC, 1, CAP), F32),
            pltpu.VMEM((NSC, 1, CAP), F32),
            pltpu.VMEM((1, CAP), F32),
            pltpu.VMEM((NSC, 1, CAP), F32),
            pltpu.VMEM((most, F), F32),
            pltpu.VMEM((most, 128), F32),
            pltpu.VMEM((most, 128), F32),
            pltpu.VMEM((NSC, 32, CAP), F32),
            pltpu.VMEM((4, 32, CAP), F32),
            pltpu.VMEM((4, 32, CAP), BF),
            pltpu.VMEM((4, 32, CAP), BF),
            pltpu.VMEM((1, CAP), F32),
            pltpu.VMEM((1, CAP), F32),
            pltpu.VMEM((1, CAP), F32),
            pltpu.VMEM((4, 1, CAP), F32),
            dma((NCP,)),
            dma((NCP,)),
            dma((NCP,)),
            dma((NCP,)),
            dma((NSC,)),
            dma((NSC,)),
            dma((NSC,)),
            dma((NSC,)),
            dma((NSC,)),
            dma((NSC,)),
            dma((parts, 5)),
            dma((parts, 5)),
            dma((parts, 4)),
            dma((parts, 4)),
            dma((parts, 4)),
            dma((parts, 4)),
            dma((NCP,)),
            dma((NCP,)),
            dma((2, NCP)),
            dma((2, NCP)),
            dma((NCP,)),
            dma((NCP,)),
            dma((2, NCP)),
            dma((2, NCP)),
            dma((2,)),
        ],
        compiler_params=pltpu.CompilerParams(
            collective_id=0, has_side_effects=True, vmem_limit_bytes=60 * 2**20
        ),
        name="main",
    )(tiles, expo_in, thr_in, factors, aversion, lengths)


def per_device(factors, loadings, thresholds, exposures, aversion, lengths):
    tiles = loadings.reshape(16, NCP, 16, F)
    load, thr, dates, risk = main(
        tiles, exposures.T, thresholds.reshape(1, ROWS), factors, aversion, lengths
    )
    return (load.T, thr.reshape(ROWS), dates.T, risk[:, 0])


def solution(mesh):
    in_specs = (P("sc", None), P("cp", None), P("cp"), P("cp", None), P(), P())
    out_specs = (P("cp", "sc"), P("cp"), P("cp", None), P())
    return jax.shard_map(
        per_device, mesh=mesh, in_specs=in_specs, out_specs=out_specs, check_vma=False
    )
```

```python
import math

import jax
import jax.numpy as jnp
from jax import lax
from jax.experimental import pallas as pl
from jax.experimental.pallas import tpu as pltpu
from jax.sharding import PartitionSpec as P

MESH = pl.DeviceIdType.MESH
NCP = 16
NSC = 8
F = 256
ROWS = 4096
S = 4096
CAP = 2176
SEG = ROWS // NCP
LIVE = 32768
SCEN = 32768
ST = 512
CHUNKS = ((0, 896), (896, 768), (1664, 512))
ROOT_HALF = 0.7071067811865476
LOG2E = 1.4426950408889634
FAR = -3.1
TAIL = (-0.750217616, 0.756257034, -1.37553279, 0.0025935648)
KEPT = 1
BF = jnp.bfloat16
F32 = jnp.float32


def spots(lengths_ref, position):
    low, high = [], []
    at = jnp.int32(0)
    beyond = jnp.int32(0)
    for block in range(NCP):
        offset = (position - block + NCP) % NCP
        tiles = (((lengths_ref[block] + 15) >> 4) - offset + 15) >> 4
        low.append(at)
        high.append(beyond)
        at = at + jnp.minimum(tiles, 8)
        beyond = beyond + jnp.maximum(tiles - 8, 0)
    return low, [at + place for place in high], at


def double_cdf(u):
    far = TAIL[3]
    for coef in TAIL[2::-1]:
        far = far * u + coef
    return jnp.where(u < FAR, jnp.exp2(far), 1.0 + lax.erf(u))


def run(first, last, act):
    def body(k, _):
        act(k)
        return 0

    lax.fori_loop(first, last, body, 0)


def main_kernel(
    tiles, expo_in, thr_in, factors, aversion, lengths, load_out, thr_out, expo_out, risk,
    got, got_high, small, got_small, wide, comp, shift, slope, expo, expo_t, table, lives, begins, kept, full, pack, back, prob, loss, parts, mine, every, stats, weights, turned,
    expo_acc, dates, dates_in, date_sum, date_all,
    load_acc, lat_acc, thr_acc, grads, pair, sum_l, near_l, thr_line, thr_pair, thr_sum, thr_near,
    sends, recvs, sends_g, recvs_g, sends_z, recvs_z, sends_d, recvs_d, sends_e, recvs_e,
    sends_a, recvs_a, sends_b, recvs_b, sends_t, recvs_t, sends_c, recvs_c,
    sends_x, recvs_x, sends_s, recvs_s, sends_y, recvs_y, own,
):
    me = lax.axis_index("cp")
    sc = lax.axis_index("sc")
    core = sc % 2
    z = sc // 2
    sibling = sc + 1 - 2 * core
    width = S // NCP
    barrier = pltpu.get_barrier_semaphore()
    run(1, NCP, lambda k: pl.semaphore_signal(barrier, inc=1, device_id=((me + k) % NCP, sc), device_id_type=MESH))
    run(1, NSC, lambda k: pl.semaphore_signal(barrier, inc=1, device_id=(me, (sc + k) % NSC), device_id_type=MESH))

    def remote(src, dst, send, recv, to):
        return pltpu.make_async_remote_copy(
            src_ref=src, dst_ref=dst, send_sem=send, recv_sem=recv, device_id=to, device_id_type=MESH
        )

    half = core * 4

    def row_copy(k, high):
        peer = (me + k) % NCP
        return remote(
            tiles.at[pl.ds(8 * high + half, 4), (peer - me + NCP) % NCP],
            (got, got_high)[high].at[pl.ds(me * 8 + half, 4)],
            sends_x.at[high, k], recvs_x.at[high, k], (peer, sc),
        )

    def small_copy(k):
        peer = (me + k) % NCP
        return remote(
            small.at[(peer - me + NCP) % NCP], got_small.at[me], sends_s.at[k], recvs_s.at[k], (peer, sc)
        )

    def pass_on(k, high):
        at = pl.ds(((me - k + NCP) % NCP) * 8 + half, 4)
        part = (got, got_high)[high].at[at]
        return remote(part, part, sends_y.at[high, k], recvs_y.at[high, k], (me, sibling))

    def own_copy(high):
        return pltpu.make_async_copy(
            tiles.at[pl.ds(8 * high, 8), 0], (got, got_high)[high].at[pl.ds(me * 8, 8)], own.at[high]
        )

    chunk_of = lax.broadcasted_iota(jnp.int32, (16, 128), 1) // 16
    limits = jnp.broadcast_to(thr_in[...].astype(F32).reshape(1, ROWS), (8, ROWS))
    raw = jnp.concatenate([expo_in[...].astype(F32), limits], axis=0)
    for t in range(NCP):
        for h in range(2):
            mixed = None
            for q in range(8):
                tile = 2 * (8 * h + q) + t // 8
                moved = pltpu.roll(raw[:, 128 * tile : 128 * (tile + 1)], (16 * (q - t % 8)) % 128, 1)
                mixed = moved if mixed is None else jnp.where(chunk_of == q, moved, mixed)
            small[t, :, 128 * h : 128 * (h + 1)] = mixed.astype(BF)

    pl.semaphore_wait(barrier, NCP + NSC - 2)
    run(1, NCP, lambda k: (small_copy(k).start(), row_copy(k, 0).start()))
    own_copy(0).start()
    run(1, NCP, lambda k: row_copy(k, 1).start())
    own_copy(1).start()
    got_small[me] = small[0]

    low, high, lows = spots(lengths, me)
    for block in range(NCP):
        begins[block] = low[block]
        begins[NCP + block] = high[block]

    def tabulate(k):
        block_low = jnp.int32(0)
        block_high = jnp.int32(0)
        for i in range(1, NCP):
            block_low = block_low + jnp.where(k >= begins[i], 1, 0)
            block_high = block_high + jnp.where(k >= begins[NCP + i], 1, 0)
        slot_low = jnp.clip(k - begins[block_low], 0, 7)
        past = k - begins[NCP + block_high]
        slot_high = jnp.clip(past, 0, 7)
        upper = k >= lows
        block = jnp.where(upper, block_high, block_low)
        slot = jnp.where(upper, slot_high + 8, slot_low)
        table[0, k] = block_low * 8 + slot_low
        table[1, k] = block_high * 8 + slot_high
        table[2, k] = block * 16 + slot
        table[3, k] = jnp.where(upper, 1, 0)
        offset = (me - block + NCP) & 15
        spare = jnp.where(upper & (past > 7), 32768, 0)
        lives[k] = lengths[block] - (offset + 16 * slot) * 16 - spare

    run(0, CAP // 16, tabulate)
    run(1, NCP, lambda k: small_copy(k).wait_recv())
    for block in range(NCP):
        part = got_small[block].astype(F32)
        part = jnp.concatenate([part, jnp.zeros((112, SEG), F32)], axis=0).T
        for slot in range(16):
            wide[block * 16 + slot] = part[16 * slot : 16 * (slot + 1), :]
    run(1, NCP, lambda k: (row_copy(k, 0).wait_recv(), pass_on(k, 0).start()))
    own_copy(0).wait()
    run(1, NCP, lambda k: pass_on(k, 0).wait_recv())

    row_of = lax.broadcasted_iota(jnp.int32, (16, 128), 0)
    lane_of = lax.broadcasted_iota(jnp.int32, (16, 128), 1)

    def compact(i, mixed):
        at = pl.ds(pl.multiple_of(i * 128, 128), 128)
        pieces = []
        for q in range(8):
            piece = got[table[0, 8 * i + q]].astype(F32)
            if mixed:
                upper = jnp.full((16, F), table[3, 8 * i + q], jnp.int32) > 0
                piece = jnp.where(upper, got_high[table[1, 8 * i + q]].astype(F32), piece)
            pieces.append(piece)
        rows = jnp.concatenate(pieces, axis=0)
        part = jnp.concatenate(
            [
                jnp.where((row_of < lives[8 * i + q]) | (lane_of >= 8), wide[table[2, 8 * i + q]], 0.0)
                for q in range(8)
            ],
            axis=0,
        )
        comp[at, :] = rows.astype(BF)
        total = jnp.sum(rows * rows, axis=1, keepdims=True)
        by = lax.rsqrt(1.0 + total) * ROOT_HALF
        slope[at, :] = jnp.broadcast_to(by, (128, 128))
        shift[at, :] = jnp.broadcast_to(part[:, 8:9] * by, (128, 128))
        expo[at, :] = part.astype(BF)
        expo_t[:, at] = part.T[0:16, :].astype(BF)

    def latent(first, count, cols):
        rows = pl.ds(first, count)
        project = lax.dot_general(
            comp[rows, :], factors[cols, :], (((1,), (1,)), ((), ())), preferred_element_type=F32
        )
        a = jnp.concatenate([shift[rows, :]] * (ST // 128), axis=1)
        b = jnp.concatenate([slope[rows, :]] * (ST // 128), axis=1)
        return a - project * b

    def ahead(step, parts_of):
        cols = pl.ds(pl.multiple_of(step * ST, ST), ST)
        for first, count in parts_of:
            u = latent(first, count, cols)
            if (first, count) == CHUNKS[KEPT]:
                kept[:, cols] = u
            prob[pl.ds(first, count), cols] = double_cdf(u).astype(BF)

    def ahead_pass(step):
        ahead(step, CHUNKS[:1])
        for j in range(3):
            k = 1 + (step - 2) * 3 + j
            row_copy(k, 1).wait_recv()
            pass_on(k, 1).start()

    def ahead_rest(step):
        cols = pl.ds(pl.multiple_of(step * ST, ST), ST)
        ahead(step, CHUNKS[1:])
        loss[:, cols] = jnp.dot(expo_t[...], prob[:, cols], preferred_element_type=F32)[0:8, :]

    run(0, CHUNKS[0][1] // 128, lambda i: compact(i, False))
    run(0, 2, lambda step: ahead(step, CHUNKS[:1]))
    run(2, 7, ahead_pass)
    run(7, S // ST, lambda step: ahead(step, CHUNKS[:1]))
    own_copy(1).wait()
    run(1, NCP, lambda k: pass_on(k, 1).wait_recv())
    run(CHUNKS[0][1] // 128, CAP // 128, lambda i: compact(i, True))
    run(0, S // ST, ahead_rest)
    run(1, NCP, lambda k: (row_copy(k, 0).wait_send(), row_copy(k, 1).wait_send(), small_copy(k).wait_send()))
    run(1, NCP, lambda k: (pass_on(k, 0).wait_send(), pass_on(k, 1).wait_send()))

    def part_of(position):
        return pl.ds(pl.multiple_of(position * width, width), width)

    def scatter(k):
        peer = (me + k) % NCP
        return remote(loss.at[:, part_of(peer)], parts.at[me], sends.at[k], recvs.at[k], (peer, sc))

    def gather(k):
        return remote(mine, every.at[:, part_of(me)], sends_g.at[k], recvs_g.at[k], ((me + k) % NCP, sc))

    def share(k):
        return remote(stats.at[sc], stats.at[sc], sends_z.at[k], recvs_z.at[k], (me, (sc + k) % NSC))

    run(1, NCP, lambda k: scatter(k).start())
    parts[me] = loss[:, part_of(me)]
    at_date = lax.broadcasted_iota(jnp.int32, (8, 128), 0)
    averse = jnp.zeros((8, 128), F32)
    for t in range(8):
        averse = jnp.where(at_date == t, aversion[t], averse)
    run(1, NCP, lambda k: scatter(k).wait_recv())
    total = parts[0]
    for i in range(1, NCP):
        total = total + parts[i]
    score = jnp.concatenate([averse] * (width // 128), axis=1) * (total * (0.5 / LIVE))
    mine[...] = score
    run(1, NCP, lambda k: gather(k).start())
    every[:, part_of(me)] = score
    run(1, NCP, lambda k: gather(k).wait_recv())
    scores = every[...]
    top = jnp.max(scores, axis=1, keepdims=True)
    raised = jnp.exp(scores - top)
    mass = jnp.sum(raised, axis=1, keepdims=True)
    stats[sc, 0:8, :] = jnp.broadcast_to(top, (8, 128))
    stats[sc, 8:16, :] = jnp.broadcast_to(mass, (8, 128))
    run(1, NSC, lambda k: share(k).start())
    weights[...] = jnp.concatenate([raised, jnp.zeros((8, S), F32)], axis=0).astype(BF)

    expo_acc[...] = jnp.zeros_like(expo_acc)

    def expose(step):
        cols = pl.ds(pl.multiple_of(step * ST, ST), ST)
        turned[:, 0:16] = weights[:, cols].astype(F32).T.astype(BF)
        expo_acc[...] += jnp.dot(prob[:, cols], turned[:, 0:16], preferred_element_type=F32)

    run(0, S // ST, expose)
    run(1, NSC, lambda k: share(k).wait_recv())
    best = stats[0, 0:8, :]
    for i in range(1, NSC):
        best = jnp.maximum(best, stats[i, 0:8, :])
    heap = jnp.zeros((8, 128), F32)
    for i in range(NSC):
        heap = heap + stats[i, 8:16, :] * jnp.exp(stats[i, 0:8, :] - best)
    final = jnp.exp(every[...] - best[:, 0:1]) / heap[:, 0:1]
    weights[...] = jnp.concatenate([final, jnp.zeros((8, S), F32)], axis=0).astype(BF)
    risk[...] = (best + jnp.log(heap / SCEN)) / averse
    run(1, NCP, lambda k: scatter(k).wait_send())
    run(1, NCP, lambda k: gather(k).wait_send())
    run(1, NSC, lambda k: share(k).wait_send())
    own_scale = jnp.exp(stats[sc, 0:8, :] - best) / heap * (0.5 / LIVE)
    for i in range(CAP // 128):
        block = jnp.concatenate(
            [expo_acc[128 * i : 128 * (i + 1), :], jnp.zeros((128, 112), F32)], axis=1
        ).T
        for j in range(NSC):
            dates[j, :, 128 * i : 128 * (i + 1)] = block[j : j + 1, :] * own_scale[j : j + 1, :]

    def date_out(k):
        peer = (sc + k) % NSC
        return remote(dates.at[peer], dates_in.at[k], sends_d.at[k], recvs_d.at[k], (me, peer))

    def date_share(k):
        return remote(date_sum, date_all.at[sc], sends_e.at[k], recvs_e.at[k], (me, (sc + k) % NSC))

    run(1, NSC, lambda k: date_out(k).start())

    def pair_copy(c, k):
        first, count = CHUNKS[c]
        at = pl.ds(first, count)
        return remote(
            grads.at[((z + k) % 4) * 2 + 1 - core, :, at], pair.at[k, :, at],
            sends_a.at[c, k], recvs_a.at[c, k], (me, sibling),
        )

    def thr_pair_copy(c):
        at = pl.ds(*CHUNKS[c])
        return remote(thr_line.at[:, at], thr_pair.at[:, at], sends_a.at[c, 4], recvs_a.at[c, 4], (me, sibling))

    def near_copy(c, k):
        at = pl.ds(*CHUNKS[c])
        return remote(
            sum_l.at[k, :, at], near_l.at[k, :, at],
            sends_b.at[c, k], recvs_b.at[c, k], (me, ((z + k) % 4) * 2 + core),
        )

    def thr_near_copy(c, k):
        at = pl.ds(*CHUNKS[c])
        return remote(
            thr_sum.at[:, at], thr_near.at[k, :, at],
            sends_t.at[c, k], recvs_t.at[c, k], (me, ((z + k) % 4) * 2 + core),
        )

    def back_steps(c, low, high):
        first, count = CHUNKS[c]
        rows = pl.ds(first, count)
        acc = pl.ds(0, count)

        def step(i):
            cols = pl.ds(pl.multiple_of(i * ST, ST), ST)
            pull = jnp.dot(expo[rows, 0:16], weights[:, cols], preferred_element_type=F32)
            u = kept[:, cols] if c == KEPT else latent(first, count, cols)
            heavy = pull * jnp.exp2(u * u * (-LOG2E))
            lat = heavy * u
            lat_sum = lat[:, 0:128]
            thr_part = heavy[:, 0:128]
            for k in range(1, ST // 128):
                lat_sum = lat_sum + lat[:, k * 128 : (k + 1) * 128]
                thr_part = thr_part + heavy[:, k * 128 : (k + 1) * 128]
            lat_acc[acc, :] += lat_sum
            thr_acc[acc, :] += thr_part
            load_acc[acc, :] += jnp.dot(heavy.astype(BF), factors[cols, :], preferred_element_type=F32)

        run(low, high, step)

    def fold(c):
        first, count = CHUNKS[c]
        scale = 1.0 / (LIVE * math.sqrt(2.0 * math.pi))

        def one(i):
            rows = pl.ds(pl.multiple_of(first + i * 128, 128), 128)
            acc = pl.ds(pl.multiple_of(i * 128, 128), 128)
            by = slope[rows, 0:1] * math.sqrt(2.0)
            lat = jnp.sum(lat_acc[acc, :], axis=1, keepdims=True) * (scale * math.sqrt(2.0))
            thr = jnp.sum((thr_acc[acc, :] * (scale * by)).T, axis=0, keepdims=True)
            grad = -(load_acc[acc, :] * (scale * by)) - (lat * by * by) * comp[rows, :].astype(F32)
            flat = grad.T
            for j in range(NSC):
                grads[j, :, rows] = flat[32 * j : 32 * (j + 1), :]
            thr_line[:, rows] = thr

        run(0, count // 128, one)
        for k in (2, 1, 3, 0):
            pair_copy(c, k).start()
        thr_pair_copy(c).start()

    def pair_up(c):
        first, count = CHUNKS[c]
        at = pl.ds(first, count)
        for k in (2, 1, 3):
            pair_copy(c, k).wait_recv()
            sum_l[k, :, at] = (grads[((z + k) % 4) * 2 + core, :, at] + pair[k, :, at]).astype(BF)
            near_copy(c, k).start()
        thr_pair_copy(c).wait_recv()
        thr_sum[:, at] = thr_line[:, at] + thr_pair[:, at]
        for k in (2, 1, 3):
            thr_near_copy(c, k).start()
        pair_copy(c, 0).wait_recv()

    def near_up(c):
        first, count = CHUNKS[c]
        at = pl.ds(first, count)
        held = grads[sc, :, at] + pair[0, :, at]
        thr = thr_sum[:, at]
        for k in (1, 3, 2):
            near_copy(c, k).wait_recv()
            thr_near_copy(c, k).wait_recv()
            held = held + near_l[k, :, at].astype(F32)
            thr = thr + thr_near[k, :, at]
        for i in range(count // 128):
            part = slice(128 * i, 128 * (i + 1))
            full[first // 128 + i, 0:32, :] = held[:, part]
            full[first // 128 + i, 40:41, :] = thr[:, part]

    full[CAP // 128 :, :, :] = jnp.zeros((3, 48, 128), F32)
    full[0 : CAP // 128, 40:48, :] = jnp.zeros((CAP // 128, 8, 128), F32)
    steps = S // ST
    for c in range(len(CHUNKS)):
        load_acc[...] = jnp.zeros_like(load_acc)
        lat_acc[...] = jnp.zeros_like(lat_acc)
        thr_acc[...] = jnp.zeros_like(thr_acc)
        back_steps(c, 0, steps // 2)
        if c == 0:
            run(1, NSC, lambda k: date_out(k).wait_recv())
            line = dates[sc]
            for k in range(1, NSC):
                line = line + dates_in[k]
            date_sum[...] = line
            run(1, NSC, lambda k: date_share(k).start())
            date_all[sc] = line
        else:
            pair_up(c - 1)
        back_steps(c, steps // 2, steps)
        if c:
            near_up(c - 1)
        fold(c)
    last = len(CHUNKS) - 1
    run(1, NSC, lambda k: date_share(k).wait_recv())
    for j in range(NSC):
        for i in range(CAP // 128):
            full[i, 32 + j : 33 + j, :] = date_all[j, :, 128 * i : 128 * (i + 1)]
    pair_up(last)
    run(1, NSC, lambda k: (date_out(k).wait_send(), date_share(k).wait_send()))
    near_up(last)
    lane = lax.broadcasted_iota(jnp.int32, (48, 128), 1)
    for block in range(NCP):
        offset = (me - block + NCP) % NCP
        for upper, start in ((0, low[block]), (1, high[block])):
            tile = start >> 3
            piece = jnp.concatenate([full[tile], full[tile + 1]], axis=1)
            part = jnp.full((48, 256), start & 7, jnp.int32)
            for bit in (1, 2, 4):
                piece = jnp.where(part & bit != 0, pltpu.roll(piece, 256 - 16 * bit, 1), piece)
            row = (offset + 16 * (8 * upper + lane // 16)) * 16 + lane % 16
            pack[block, :, 128 * upper : 128 * (upper + 1)] = jnp.where(
                row < lengths[block], piece[:, 0:128], 0.0
            ).astype(BF)

    def back_copy(k):
        peer = (me + k) % NCP
        return remote(pack.at[peer], back.at[(me - peer + NCP) % NCP], sends_c.at[k], recvs_c.at[k], (peer, sc))

    run(1, NCP, lambda k: back_copy(k).start())
    back[0] = pack[me]
    for c in range(len(CHUNKS)):
        for k in range(4):
            pair_copy(c, k).wait_send()
        thr_pair_copy(c).wait_send()
        for k in range(1, 4):
            near_copy(c, k).wait_send()
            thr_near_copy(c, k).wait_send()
    run(1, NCP, lambda k: back_copy(k).wait_recv())
    group = lax.broadcasted_iota(jnp.int32, (48, 128), 1) // 16
    for g in range(2):
        for h in range(2):
            held = [back[8 * g + q, :, 128 * h : 128 * (h + 1)].astype(F32) for q in range(8)]
            for s in range(8):
                mixed = held[s]
                for q in range(8):
                    if q != s:
                        moved = pltpu.roll(held[q], (16 * (q - s)) % 128, 1)
                        mixed = jnp.where(group == q, moved, mixed)
                tile = 2 * (8 * h + s) + g
                at = slice(128 * tile, 128 * (tile + 1))
                load_out[:, at] = mixed[0:32, :]
                expo_out[:, at] = mixed[32:40, :]
                thr_out[:, at] = mixed[40:41, :]
    run(1, NCP, lambda k: back_copy(k).wait_send())


def main(tiles, expo_in, thr_in, factors, aversion, lengths):
    vmem = pl.BlockSpec(memory_space=pltpu.VMEM)
    dma = pltpu.SemaphoreType.DMA
    parts = len(CHUNKS)
    most = max(count for _, count in CHUNKS)
    return pl.pallas_call(
        main_kernel,
        out_shape=(
            jax.ShapeDtypeStruct((32, ROWS), F32),
            jax.ShapeDtypeStruct((1, ROWS), F32),
            jax.ShapeDtypeStruct((NSC, ROWS), F32),
            jax.ShapeDtypeStruct((8, 128), F32),
        ),
        in_specs=[pl.BlockSpec(memory_space=pl.ANY)] + [vmem] * 3 + [pl.BlockSpec(memory_space=pltpu.SMEM)] * 2,
        out_specs=[vmem] * 4,
        scratch_shapes=[
            pltpu.VMEM((NCP * 8, 16, F), BF),
            pltpu.VMEM((NCP * 8, 16, F), BF),
            pltpu.VMEM((NCP, 16, SEG), BF),
            pltpu.VMEM((NCP, 16, SEG), BF),
            pltpu.VMEM((NCP * 16, 16, 128), F32),
            pltpu.VMEM((CAP, F), BF),
            pltpu.VMEM((CAP, 128), F32),
            pltpu.VMEM((CAP, 128), F32),
            pltpu.VMEM((CAP, 128), BF),
            pltpu.VMEM((16, CAP), BF),
            pltpu.SMEM((4, CAP // 16), jnp.int32),
            pltpu.SMEM((CAP // 16,), jnp.int32),
            pltpu.SMEM((2 * NCP,), jnp.int32),
            pltpu.VMEM((CHUNKS[KEPT][1], S), F32),
            pltpu.VMEM((CAP // 128 + 3, 48, 128), F32),
            pltpu.VMEM((NCP, 48, SEG), BF),
            pltpu.VMEM((NCP, 48, SEG), BF),
            pltpu.VMEM((CAP, S), BF),
            pltpu.VMEM((8, S), F32),
            pltpu.VMEM((NCP, 8, S // NCP), F32),
            pltpu.VMEM((8, S // NCP), F32),
            pltpu.VMEM((8, S), F32),
            pltpu.VMEM((NSC, 16, 128), F32),
            pltpu.VMEM((16, S), BF),
            pltpu.VMEM((ST, 128), BF),
            pltpu.VMEM((CAP, 16), F32),
            pltpu.VMEM((NSC, 1, CAP), F32),
            pltpu.VMEM((NSC, 1, CAP), F32),
            pltpu.VMEM((1, CAP), F32),
            pltpu.VMEM((NSC, 1, CAP), F32),
            pltpu.VMEM((most, F), F32),
            pltpu.VMEM((most, 128), F32),
            pltpu.VMEM((most, 128), F32),
            pltpu.VMEM((NSC, 32, CAP), F32),
            pltpu.VMEM((4, 32, CAP), F32),
            pltpu.VMEM((4, 32, CAP), BF),
            pltpu.VMEM((4, 32, CAP), BF),
            pltpu.VMEM((1, CAP), F32),
            pltpu.VMEM((1, CAP), F32),
            pltpu.VMEM((1, CAP), F32),
            pltpu.VMEM((4, 1, CAP), F32),
            dma((NCP,)),
            dma((NCP,)),
            dma((NCP,)),
            dma((NCP,)),
            dma((NSC,)),
            dma((NSC,)),
            dma((NSC,)),
            dma((NSC,)),
            dma((NSC,)),
            dma((NSC,)),
            dma((parts, 5)),
            dma((parts, 5)),
            dma((parts, 4)),
            dma((parts, 4)),
            dma((parts, 4)),
            dma((parts, 4)),
            dma((NCP,)),
            dma((NCP,)),
            dma((2, NCP)),
            dma((2, NCP)),
            dma((NCP,)),
            dma((NCP,)),
            dma((2, NCP)),
            dma((2, NCP)),
            dma((2,)),
        ],
        compiler_params=pltpu.CompilerParams(
            collective_id=0, has_side_effects=True, vmem_limit_bytes=60 * 2**20
        ),
        name="main",
    )(tiles, expo_in, thr_in, factors, aversion, lengths)


def per_device(factors, loadings, thresholds, exposures, aversion, lengths):
    tiles = loadings.reshape(16, NCP, 16, F)
    load, thr, dates, risk = main(
        tiles, exposures.T, thresholds, factors, aversion, lengths
    )
    return (load.T, thr.reshape(ROWS), dates.T, risk[:, 0])


def solution(mesh):
    in_specs = (P("sc", None), P("cp", None), P("cp"), P("cp", None), P(), P())
    out_specs = (P("cp", "sc"), P("cp"), P("cp", None), P())
    return jax.shard_map(
        per_device, mesh=mesh, in_specs=in_specs, out_specs=out_specs, check_vma=False
    )
```
